32 devices in a mesh: rep: 8 (over z, x), shard: 4 (over y, core).
Axes of the slice: x: 2, y: 2, z: 4, core: 2. Of those that a mesh axis runs over, the one named last changes fastest.
Arguments:
- tokens: bfloat16 [32768, 1024], P(('rep', 'shard')), may hold values from -6 to 6
- segments: int32 [32768], P(('rep', 'shard')), may hold values from 0 to 3, as said below
- norm_gain: bfloat16 [1024], P('shard'), may hold values from 0.5 to 1.5
- in_weight: bfloat16 [1024, 4352], P('shard'), may hold values from -0.1875 to 0.1875
- dt_weight: bfloat16 [1024, 32], P('shard'), may hold values from -0.1875 to 0.1875
- conv_weight: bfloat16 [2304, 4], P('shard'), may hold values from -3 to 3
- conv_bias: bfloat16 [2304], P('shard'), may hold values from -3 to 3
- dt_bias: bfloat16 [32], P('shard'), may hold values from -8 to -3
- a_log: bfloat16 [32], P('shard'), may hold values from -2 to 1.5
- d_skip: bfloat16 [32], P('shard'), may hold values from 0.5 to 1.5
- gate_gain: bfloat16 [2048], P('shard'), may hold values from 0.5 to 1.5
- out_weight: bfloat16 [2048, 1024], P('shard'), may hold values from -0.125 to 0.125
- cotangent: bfloat16 [32768, 1024], P(('rep', 'shard')), may hold values from -6 to 6
Outputs:
- output: bfloat16 [32768, 1024], P(('rep', 'shard'))
- grad_tokens: float32 [32768, 1024], P(('rep', 'shard'))
- grad_norm_gain: float32 [1024], P('shard')
- grad_in_weight: float32 [1024, 4352], P('shard')
- grad_dt_weight: float32 [1024, 32], P('shard')
- grad_conv_weight: float32 [2304, 4], P('shard')
- grad_conv_bias: float32 [2304], P('shard')
- grad_dt_bias: float32 [32], P('shard')
- grad_a_log: float32 [32], P('shard')
- grad_d_skip: float32 [32], P('shard')
- grad_gate_gain: float32 [2048], P('shard')
- grad_out_weight: float32 [2048, 1024], P('shard')
The draws below stay inside these ranges and needn't reach their ends.
Inputs may be any that keep to these rules, and one draw needn't show every extreme that they name: `segments`: within each aligned block of 4096 tokens the segment numbers run from 0 to 3 and never fall; a token belongs to the document of the tokens with its number; every document has 256 tokens or more and fewer than 2048; no quarter of a run holds more than two documents.
All inputs are finite; a program needn't handle non-finite values.
Results may differ from the reference program's by a relative error of at most 0.0087.
Values may be sent and summed in bfloat16 or wider, within the bound.
No kernel may reach another device: no remote copies, remote signals or barrier semaphores. Data moves between devices by JAX's collectives and lax.ppermute only.
A program may use at most 256 MiB of HBM per device.

```python
import jax
import jax.numpy as jnp
from jax import lax

D = 1024
HEADS = 32
HEAD_DIM = 64
STATE = 128
KW = 4
SPAN = 256
INNER = 2048
CONV = 2304
PROJ = 4352
LENGTH = 4096
TOKENS = 32768


def draw_segments(key, part):
    key = jax.random.fold_in(key, 7)
    pick_key, order_key, lead_key, trail_key, tail_key = jax.random.split(key, 5)
    seq_total = TOKENS // LENGTH
    quarter = LENGTH // 4
    seq_index = jnp.arange(seq_total)
    pattern = jax.random.randint(pick_key, (seq_total,), 0, 3)
    order = jax.random.permutation(order_key, seq_total)
    pattern = jnp.where(seq_index == order[0], 0, pattern)
    pattern = jnp.where(seq_index == order[1], 1, pattern)
    pattern = jnp.where(seq_index == order[2], 2, pattern)
    lead = jax.random.randint(lead_key, (seq_total,), quarter // 8, quarter // 2 - quarter // 32)
    trail = jax.random.randint(trail_key, (seq_total,), quarter // 8, quarter // 2 - quarter // 32)
    tail = jax.random.randint(tail_key, (seq_total,), quarter // 4, 3 * quarter // 4)
    even_cuts = jnp.stack([jnp.full((seq_total,), quarter), jnp.full((seq_total,), 2 * quarter), jnp.full((seq_total,), 3 * quarter)], axis=1)
    early_cuts = jnp.stack([quarter - lead, 2 * quarter + trail, 3 * quarter + tail], axis=1)
    late_cuts = jnp.stack([quarter - tail, 2 * quarter - trail, 3 * quarter + lead], axis=1)
    cuts = jnp.where((pattern == 0)[:, None], even_cuts, jnp.where((pattern == 1)[:, None], early_cuts, late_cuts))
    position = jnp.arange(LENGTH)[None, :, None]
    numbers = jnp.sum((position >= cuts[:, None, :]).astype(jnp.int32), axis=2)
    return numbers.reshape(-1).astype(jnp.int32)


def block_levels(own_key, shape, cuts, least, top_value):
    def one(dim, parts):
        heights = jax.random.uniform(jax.random.fold_in(jax.random.fold_in(own_key, 6), dim), (parts,), jnp.float32, least / len(cuts), top_value / len(cuts))
        return jnp.repeat(jnp.exp(heights), shape[dim] // parts).reshape((-1,) + (1,) * (len(shape) - dim - 1))

    factor_of = one(*cuts[0])
    for cut in cuts[1:]:
        factor_of = factor_of * one(*cut)
    return factor_of


def centred(rng, extent, deviation, limit, shards=(), held_as=jnp.bfloat16):
    entries = jax.random.normal(rng, extent, jnp.float32) * deviation
    if len(shards) > 0:
        entries = block_levels(rng, extent, shards, -0.22, 0.18) * entries
    return jnp.clip(entries, min=-limit, max=limit).astype(held_as)


def setup_inputs(seed: int = 0) -> dict:
    key_list = jax.random.split(jax.random.key(seed), 14)
    return {
        "tokens": centred(key_list[0], (TOKENS, D), 1.0, 6.0, ((0, 32),)),
        "segments": draw_segments(jax.random.fold_in(key_list[13], 71), 0),
        "norm_gain": jnp.clip(1.0 + 0.1 * jax.random.normal(key_list[2], (D,), jnp.float32), 0.5, 1.5).astype(jnp.bfloat16),
        "in_weight": centred(key_list[3], (D, PROJ), D ** -0.5, 0.1875, ((0, 4),)),
        "dt_weight": centred(key_list[4], (D, HEADS), D ** -0.5, 0.1875, ((0, 4),)),
        "conv_weight": centred(key_list[5], (CONV, KW), KW ** -0.5, 3.0, ((0, 4),)),
        "conv_bias": centred(key_list[6], (CONV,), 0.5, 3.0, ((0, 4),)),
        "dt_bias": jnp.clip(-8.0 + 5.0 * jax.random.uniform(key_list[7], (HEADS,), jnp.float32) ** block_levels(key_list[7], (HEADS,), ((0, 4),), -0.2, 0.2), -8.0, -3.0).astype(jnp.bfloat16),
        "a_log": jnp.clip(-2.0 + 3.5 * jax.random.uniform(key_list[8], (HEADS,), jnp.float32) ** block_levels(key_list[8], (HEADS,), ((0, 4),), -0.2, 0.2), -2.0, 1.5).astype(jnp.bfloat16),
        "d_skip": jnp.clip(0.5 + 1.0 * jax.random.uniform(key_list[9], (HEADS,), jnp.float32) ** block_levels(key_list[9], (HEADS,), ((0, 4),), -0.2, 0.2), 0.5, 1.5).astype(jnp.bfloat16),
        "gate_gain": jnp.clip(1.0 + 0.1 * jax.random.normal(key_list[10], (INNER,), jnp.float32), 0.5, 1.5).astype(jnp.bfloat16),
        "out_weight": centred(key_list[11], (INNER, D), INNER ** -0.5, 0.125, ((0, 4),)),
        "cotangent": centred(key_list[12], (TOKENS, D), 1.0, 6.0, ((0, 32),)),
    }


EPSILON = 1e-05
EXACT = lax.Precision.HIGHEST

@jax.custom_vjp
def low(v):
    return lax.optimization_barrier(v.astype(jnp.bfloat16)).astype(jnp.float32)

@jax.custom_vjp
def low_back(v):
    return v

def low_keep(v):
    return (low(v), None)

def low_pass(kept, grad):
    return (grad,)

def back_keep(v):
    return (v, None)

def back_low(kept, grad):
    return (low(grad),)
low.defvjp(low_keep, low_pass)
low_back.defvjp(back_keep, back_low)

def mixer_block(carried_in, block_in):
    state_now, seg_prev = carried_in
    values, keys_in, queries, step_sizes, decays, doc_ids = block_in
    length = doc_ids.shape[0]
    position = jnp.arange(length)
    causal = (position[:, None] >= position[None, :]) & (doc_ids[:, None] == doc_ids[None, :])
    cum_decay = jnp.cumsum(decays, axis=0)
    spread = jnp.where(causal[:, :, None], cum_decay[:, None, :] - cum_decay[None, :, :], -10000.0)
    mixing = jnp.einsum('tn,sn->ts', queries, keys_in, precision=EXACT)
    weights = mixing[:, :, None] * jnp.exp(spread) * step_sizes[None, :, :]
    inside = jnp.einsum('tsh,shp->thp', weights, values, precision=EXACT)
    entry_gain = jnp.where((doc_ids == seg_prev)[:, None], jnp.exp(cum_decay), 0.0)
    carried = entry_gain[:, :, None] * jnp.einsum('tn,hpn->thp', queries, state_now, precision=EXACT)
    leaving = jnp.where((doc_ids == doc_ids[-1])[:, None], jnp.exp(cum_decay[-1][None, :] - cum_decay), 0.0) * step_sizes
    fresh_state = entry_gain[-1][:, None, None] * state_now + jnp.einsum('sh,shp,sn->hpn', leaving, values, keys_in, precision=EXACT)
    return ((fresh_state, doc_ids[-1]), inside + carried)

def layer(params, hidden, doc_ids):
    norm_gain, in_weight, dt_weight, conv_weight, conv_bias, dt_bias, a_log, d_skip, gate_gain, out_weight = params
    inv_rms = lax.rsqrt(lax.optimization_barrier(jnp.mean(hidden * hidden, axis=-1, keepdims=True)) + EPSILON)
    normed = low(hidden * inv_rms * norm_gain)
    projected = low(low_back(jnp.dot(normed, in_weight, precision=EXACT)))
    step_raw = low_back(jnp.dot(normed, dt_weight, precision=EXACT))
    gate_in = projected[:, :INNER]
    conv_in = projected[:, INNER:]
    padded = jnp.concatenate([jnp.zeros((KW - 1, CONV), jnp.float32), conv_in], axis=0)
    doc_pad = jnp.concatenate([jnp.full((KW - 1,), -1, jnp.int32), doc_ids])
    conv_sum = conv_bias
    for offset in range(KW):
        same_doc = (doc_pad[offset:offset + LENGTH] == doc_ids)[:, None]
        conv_sum = conv_sum + conv_weight[:, offset] * jnp.where(same_doc, padded[offset:offset + LENGTH], 0.0)
    active = jax.nn.silu(conv_sum)
    values = active[:, :INNER].reshape(LENGTH, HEADS, HEAD_DIM)
    keys_in = active[:, INNER:INNER + STATE]
    queries = active[:, INNER + STATE:]
    step_sizes = jax.nn.softplus(step_raw + dt_bias)
    decays = -step_sizes * jnp.exp(a_log)
    blocks = LENGTH // SPAN
    pieces = (values.reshape(blocks, SPAN, HEADS, HEAD_DIM), keys_in.reshape(blocks, SPAN, STATE), queries.reshape(blocks, SPAN, STATE), step_sizes.reshape(blocks, SPAN, HEADS), decays.reshape(blocks, SPAN, HEADS), doc_ids.reshape(blocks, SPAN))
    start_state = jnp.zeros((HEADS, HEAD_DIM, STATE), jnp.float32)
    final_carry, scanned = lax.scan(jax.checkpoint(mixer_block), (start_state, jnp.int32(-1)), pieces)
    ssd_out = scanned.reshape(LENGTH, HEADS, HEAD_DIM) + d_skip[:, None] * values
    gated = ssd_out.reshape(LENGTH, INNER) * jax.nn.silu(gate_in)
    gate_rms = lax.rsqrt(lax.optimization_barrier(jnp.mean(gated * gated, axis=-1, keepdims=True)) + EPSILON)
    mixed = low(gated * gate_rms * gate_gain)
    return hidden + jnp.dot(mixed, out_weight, precision=EXACT)

def reference(tokens, segments, norm_gain, in_weight, dt_weight, conv_weight, conv_bias, dt_bias, a_log, d_skip, gate_gain, out_weight, cotangent):
    params = (norm_gain.astype(jnp.float32), in_weight.astype(jnp.float32), dt_weight.astype(jnp.float32), conv_weight.astype(jnp.float32), conv_bias.astype(jnp.float32), dt_bias.astype(jnp.float32), a_log.astype(jnp.float32), d_skip.astype(jnp.float32), gate_gain.astype(jnp.float32), out_weight.astype(jnp.float32))
    seq_total = TOKENS // LENGTH
    inputs = (tokens.astype(jnp.float32).reshape(seq_total, LENGTH, D), segments.reshape(seq_total, LENGTH), cotangent.astype(jnp.float32).reshape(seq_total, LENGTH, D))

    def one_sequence(totals, sequence):
        hidden, doc_ids, upstream = sequence
        result, pullback = jax.vjp(lambda weights, hidden_in: layer(weights, hidden_in, doc_ids), params, hidden)
        grad_weights, grad_hidden = pullback(upstream)
        totals = jax.tree.map(lambda summed, addend: summed + addend, totals, grad_weights)
        return (totals, (result.astype(jnp.bfloat16), grad_hidden))
    zero_grads = jax.tree.map(jnp.zeros_like, params)
    totals, (results, input_grads) = lax.scan(one_sequence, zero_grads, inputs)
    g_norm, g_in, g_dt, g_conv, g_cbias, g_dbias, g_alog, g_skip, g_gate, g_out = totals
    return (results.reshape(TOKENS, D), input_grads.reshape(TOKENS, D), g_norm, g_in, g_dt, g_conv, g_cbias, g_dbias, g_alog, g_skip, g_gate, g_out)
```

```python
from functools import partial

import jax
import jax.numpy as jnp
from jax import lax
from jax.experimental import pallas as pl
from jax.experimental.pallas import tpu as pltpu
from jax.sharding import PartitionSpec as P

HEADS = 32
HEAD_DIM = 64
STATE = 128
KW = 4
SPAN = 256
INNER = 2048
GROUP = 4
WIDE = GROUP * HEAD_DIM
GROUPS = HEADS // GROUP
ORDER = (0, 2, 1, 3)
CALLS = 4
PER_CALL = GROUPS // CALLS
HALO = 16
CUT = -200.0
EPSILON = 1e-05
EXACT = lax.Precision.HIGHEST
BF = jnp.bfloat16
F32 = jnp.float32
VMEM = 56 * 1024 * 1024


def params():
    return pltpu.CompilerParams(vmem_limit_bytes=VMEM)


def cost(micros):
    return pl.CostEstimate(flops=int(micros * 2.0e7), bytes_accessed=0, transcendentals=0)


def mm(a, b):
    return jnp.dot(a, b, preferred_element_type=F32)


def mm_nt(a, b):
    return lax.dot_general(a, b, (((1,), (1,)), ((), ())), preferred_element_type=F32)


def mm_tn(a, b):
    return lax.dot_general(a, b, (((0,), (0,)), ((), ())), preferred_element_type=F32)


def iota(shape, dim):
    return lax.broadcasted_iota(jnp.int32, shape, dim)


def own_lanes(full, step):
    return pltpu.roll(full, lax.rem(128 - GROUP * step, 128), 1)


def pick_heads(step):
    row, col = iota((128, WIDE), 0), iota((128, WIDE), 1)
    wanted = GROUP * step + col // HEAD_DIM
    return jnp.where((row == wanted) | (row == wanted + HEADS), 1.0, 0.0).astype(BF)


def sum_heads(step):
    row, col = iota((WIDE, 128), 0), iota((WIDE, 128), 1)
    return jnp.where(GROUP * step + row // HEAD_DIM == col, 1.0, 0.0).astype(BF)


def two_parts(value):
    value = jnp.where(iota(value.shape, 1) < HEADS, value, 0.0)
    high = value.astype(BF).astype(F32)
    return (high + pltpu.roll(value - high, HEADS, 1)).astype(BF)


def tri(lower):
    a, b = iota((SPAN, SPAN), 0), iota((SPAN, SPAN), 1)
    return (a >= b) if lower else (a <= b)


def norm_kernel(me_ref, edge_ref, tokens_ref, gain_ref, keep_ref, give_ref, plain_ref):
    rows, model = tokens_ref.shape
    quarter = model // 4
    me = me_ref[0]

    def one(ref, start, size, out):
        hidden = ref[pl.ds(start, size), :].astype(F32)
        inv = lax.rsqrt(jnp.mean(hidden * hidden, axis=-1, keepdims=True) + EPSILON)
        for place, flip in enumerate(ORDER):
            at = pl.ds(pl.multiple_of((me ^ flip) * quarter, quarter), quarter)
            part = ref[pl.ds(start, size), at].astype(F32) * inv * gain_ref[:, at]
            target = keep_ref if place < 2 else give_ref
            cols = pl.ds((place % 2) * quarter, quarter)
            target[pl.ds(out, size), cols] = part.astype(BF)
            if out >= HALO:
                plain_ref[pl.ds(start, size), at] = part.astype(BF)

    one(edge_ref, 0, HALO, 0)
    for c in range(rows // SPAN):
        one(tokens_ref, c * SPAN, SPAN, HALO + c * SPAN)


def project(xk_ref, xg_ref, w_refs, start, size):
    quarter = xk_ref.shape[1] // 2
    at = pl.ds(start, size)
    total = None
    for place, flip in enumerate(ORDER):
        x_ref = xk_ref if place < 2 else xg_ref
        part = mm(x_ref[at, pl.ds((place % 2) * quarter, quarter)], w_refs[flip][...])
        total = part if total is None else total + part
    return total


def conv_rows(p_ref, taps_ref, masks, c):
    total = jnp.broadcast_to(taps_ref[KW : KW + 1, :], (SPAN, p_ref.shape[1]))
    base = HALO - KW + 1 + c * SPAN
    for k in range(KW):
        part = taps_ref[k : k + 1, :] * p_ref[pl.ds(base + k, SPAN), :]
        if k < KW - 1:
            part = part * masks[:, k : k + 1]
        total = total + part
    return total


def project_conv(xk_ref, xg_ref, w_refs, taps_ref, masks_ref, proj_ref, act_ref, slope_ref, p_ref, c):
    at = pl.ds(c * SPAN, SPAN)
    up = pl.ds(HALO + c * SPAN, SPAN)
    if c == 0:
        edge = project(xk_ref, xg_ref, w_refs, 0, HALO).astype(BF)
        proj_ref[pl.ds(0, HALO), :] = edge
        p_ref[pl.ds(0, HALO), :] = edge.astype(F32)
    own = project(xk_ref, xg_ref, w_refs, HALO + c * SPAN, SPAN).astype(BF)
    proj_ref[up, :] = own
    p_ref[up, :] = own.astype(F32)
    cs = conv_rows(p_ref, taps_ref, masks_ref[up, :], c)
    sig = jax.nn.sigmoid(cs)
    act = cs * sig
    act_ref[at, :] = act.astype(BF)
    slope_ref[at, :] = (sig * (1.0 + cs - act)).astype(BF)
    return act


def first_kernel(
    xk_ref, xg_ref, w0, w1, w2, w3, d0, d1, d2, d3, taps_ref, hp_ref, docs_ref,
    proj_ref, act_ref, slope_ref, turned_ref, raw_ref, step_ref, cum_ref, cumt_ref, mix_ref,
    mixt_ref, masks_ref, run_ref, step2_ref, enter2_ref, leave2_ref, p_ref,
):
    rows = act_ref.shape[0]
    ext = rows + HALO
    lower = tri(True)
    ones_lower = jnp.where(lower, 1.0, 0.0).astype(F32)
    here = docs_ref[pl.ds(8, ext), :]
    lane = iota((ext, 8), 1)
    inside = iota((ext, 1), 0) - HALO
    masks = jnp.zeros((ext, 8), F32)
    for k in range(KW - 1):
        back = docs_ref[pl.ds(8 - KW + 1 + k, ext), :] == here
        masks = masks + jnp.where((lane == k) & back, 1.0, 0.0)
        ahead = (docs_ref[pl.ds(8 + KW - 1 - k, ext), :] == here) & (inside + KW - 1 - k >= 0)
        masks = masks + jnp.where((lane == 4 + k) & ahead, 1.0, 0.0)
    masks_ref[...] = masks
    total = jnp.zeros((1, 128), F32)
    for c in range(rows // SPAN):
        at = pl.ds(c * SPAN, SPAN)
        up = pl.ds(HALO + c * SPAN, SPAN)
        act = project_conv(
            xk_ref, xg_ref, (w0, w1, w2, w3), taps_ref, masks_ref, proj_ref, act_ref, slope_ref,
            p_ref, c,
        )
        turned_ref[:, at] = act.T.astype(BF)
        act = act.astype(BF)
        keys, queries = act[:, :STATE], act[:, STATE:]
        mix_ref[c] = jnp.where(lower, mm_nt(queries, keys), 0.0)
        mixt_ref[c] = jnp.where(tri(False), mm_nt(keys, queries), 0.0)
        quarter = xk_ref.shape[1] // 2
        raw = jnp.zeros((SPAN, 128), F32)
        for place, flip in enumerate(ORDER):
            x_ref = xk_ref if place < 2 else xg_ref
            part = x_ref[up, pl.ds((place % 2) * quarter, quarter)]
            raw = raw + mm_nt(part, (d0, d1, d2, d3)[flip][pl.ds(0, 128), pl.ds(0, quarter)])
        raw_ref[at, :] = raw
        step = jax.nn.softplus(raw + hp_ref[0:1, :])
        step_ref[at, :] = step
        cut = 1.0 - masks_ref[up, KW - 2 : KW - 1]
        decays = -step * jnp.exp(hp_ref[1:2, :]) + CUT * cut
        cum = jnp.dot(ones_lower, decays, precision=EXACT, preferred_element_type=F32)
        cum_ref[at, :] = cum
        cumt = lax.dot_general(
            decays, ones_lower, (((0,), (1,)), ((), ())), precision=EXACT,
            preferred_element_type=F32,
        )
        for g in range(GROUPS):
            cumt_ref[g, :, at] = cumt[GROUP * g : GROUP * (g + 1), :]
        end = cum[SPAN - 1 : SPAN, :]
        total = total + end
        step2_ref[at, :] = two_parts(step)
        enter2_ref[at, :] = two_parts(jnp.exp(cum))
        leave2_ref[at, :] = two_parts(jnp.exp(end - cum))
    run_ref[...] = jnp.broadcast_to(total, (8, 128))


def gain_row(cum_row, step):
    return mm(two_parts(jnp.exp(jnp.broadcast_to(cum_row, (16, 128)))), pick_heads(step))[0:1, :]


def state_kernel(
    xk_ref, xg_ref, w0, w1, w2, w3, taps_ref, masks_ref, step2_ref, leave2_ref, cum_ref, turned_ref,
    proj_ref, act_ref, slope_ref, add_ref, last_ref, p_ref,
):
    rows = act_ref.shape[0]
    i = pl.program_id(0)
    pick = pick_heads(i)
    state = jnp.zeros((STATE, WIDE), F32)
    for c in range(rows // SPAN):
        at = pl.ds(c * SPAN, SPAN)
        act = project_conv(
            xk_ref, xg_ref, (w0, w1, w2, w3), taps_ref, masks_ref, proj_ref, act_ref, slope_ref,
            p_ref, c,
        )
        scale = mm(step2_ref[at, :], pick) * mm(leave2_ref[at, :], pick)
        new = mm(turned_ref[pl.ds(0, STATE), at], (act * scale).astype(BF))
        add_ref[c] = new.astype(BF)
        end = cum_ref[pl.ds(c * SPAN + SPAN - 1, 1), :]
        state = gain_row(end, i) * state + new
    last_ref[...] = state.astype(BF)


def inside_kernel(
    xk_ref, xg_ref, w0, w1, w2, w3, act_ref, step2_ref, cum_ref, cumt_ref, mix_ref, hp_ref,
    y_ref, gate_ref,
):
    rows = act_ref.shape[0]
    i = pl.program_id(0)
    low = iota((SPAN, 128), 1) < HEAD_DIM
    pick = pick_heads(i)
    skip = mm(two_parts(jnp.broadcast_to(hp_ref[2:3, :], (16, 128))), pick)[0:1, :]
    for c in range(rows // SPAN):
        at = pl.ds(c * SPAN, SPAN)
        gate_ref[at, :] = project(
            xk_ref, xg_ref, (w0, w1, w2, w3), HALO + c * SPAN, SPAN
        ).astype(BF)
        cum = own_lanes(cum_ref[at, :], i)
        act = act_ref[at, :].astype(F32)
        vdt = (act * mm(step2_ref[at, :], pick)).astype(BF)
        for j in range(GROUP // 2):
            cols = slice(128 * j, 128 * (j + 1))
            pair = vdt[:, cols]
            total = skip[:, cols] * act[:, cols]
            for s in range(2):
                h = 2 * j + s
                gap = cum[:, h : h + 1] - cumt_ref[0, h : h + 1, at]
                weights = (mix_ref[c] * jnp.exp(jnp.minimum(gap, 0.0))).astype(BF)
                part = jnp.where(low if s == 0 else ~low, pair, jnp.zeros_like(pair))
                total = total + mm(weights, part)
            y_ref[at, pl.ds(128 * j, 128)] = total


def mixed_kernel(
    inside_ref, gate_ref, kq_ref, enter2_ref, cum_ref, add_ref, near_ref, far_ref, run_ref,
    gain_ref,
    y_ref, mixed_ref, rms_ref, into_ref, gated_ref, sum_ref,
):
    rows = inside_ref.shape[0]
    i = pl.program_id(0)
    pick = pick_heads(i)
    state = near_ref[...].astype(F32) + gain_row(run_ref[0:1, :], i) * far_ref[...].astype(F32)
    into_ref[...] = state

    @pl.when(i == 0)
    def _():
        sum_ref[...] = jnp.zeros_like(sum_ref)

    for c in range(rows // SPAN):
        at = pl.ds(c * SPAN, SPAN)
        y = mm(enter2_ref[at, :], pick) * mm(kq_ref[at, STATE:], state.astype(BF))
        y = y + inside_ref[at, :]
        y_ref[at, :] = y.astype(BF)
        wide = gate_ref[at, :].astype(F32)
        gated = y * (wide * jax.nn.sigmoid(wide))
        gated_ref[i, at, :] = gated
        squares = gated * gated
        sum_ref[at, :] += squares[:, :128] + squares[:, 128:]
        state = gain_row(cum_ref[pl.ds(c * SPAN + SPAN - 1, 1), :], i) * state + add_ref[c].astype(F32)

    @pl.when(i == GROUPS - 1)
    def _():
        for c in range(rows // SPAN):
            at = pl.ds(c * SPAN, SPAN)
            mean = jnp.sum(sum_ref[at, :], axis=1, keepdims=True) * (1.0 / INNER)
            rms = lax.rsqrt(mean + EPSILON)
            rms_ref[at, :] = jnp.broadcast_to(rms, (SPAN, 128))
            for g in range(GROUPS):
                cols = pl.ds(g * WIDE, WIDE)
                mixed_ref[at, cols] = (gated_ref[g, at, :] * rms * gain_ref[:, cols]).astype(BF)


def rows_kernel(me_ref, mixed_ref, tokens_ref, dgate_ref, *refs):
    wos, wgs = refs[:8], refs[8:12]
    out_ref, part_ref = refs[12:]
    me = me_ref[0]
    per = GROUPS // 4
    quarter = wgs[0].shape[0]
    total = tokens_ref[...].astype(F32)
    for flip in range(4):
        for s in range(per):
            cols = pl.ds(pl.multiple_of(((me ^ flip) * per + s) * WIDE, WIDE), WIDE)
            total = total + mm(mixed_ref[:, cols], wos[per * flip + s][...])
    out_ref[...] = total.astype(BF)
    for flip in range(4):
        own = pl.ds(pl.multiple_of((me ^ flip) * quarter, quarter), quarter)
        part_ref[:, own] = mm_nt(dgate_ref[...], wgs[flip][...])


def gate_back_kernel(
    me_ref, cot_ref, w0, w1, w2, w3, w4, w5, w6, w7, y_ref, gate_ref, rms_ref, gain_ref, act_ref,
    turned_ref, enter2_ref, cum_ref,
    dy_ref, dgate_ref, dgain_ref, dskip_ref, add_ref, first_ref, gm_ref, run_ref, acc_ref,
):
    c = pl.program_id(0)
    me = me_ref[0]

    @pl.when(c == 0)
    def _():
        dgain_ref[...] = jnp.zeros_like(dgain_ref)
        dskip_ref[...] = jnp.zeros_like(dskip_ref)
        acc_ref[...] = jnp.zeros_like(acc_ref)
        run_ref[...] = jnp.zeros_like(run_ref)

    rms = rms_ref[:, 0:1]
    total = jnp.zeros((SPAN, 128), F32)
    cot = cot_ref[...]
    per = GROUPS // 4
    ws = (w0, w1, w2, w3, w4, w5, w6, w7)
    for flip in range(4):
        for s in range(per):
            cols = pl.ds(pl.multiple_of(((me ^ flip) * per + s) * WIDE, WIDE), WIDE)
            gm = mm_nt(cot, ws[per * flip + s][...])
            gm_ref[:, cols] = gm
            wide = gate_ref[:, cols].astype(F32)
            gated = y_ref[:, cols].astype(F32) * (wide * jax.nn.sigmoid(wide))
            q = gm * gain_ref[:, cols] * gated
            total = total + q[:, :128] + q[:, 128:]
    mean = jnp.sum(total, axis=1, keepdims=True) * (1.0 / INNER)
    shrink = rms * rms * rms * mean
    for g in range(GROUPS):
        cols = pl.ds(g * WIDE, WIDE)
        pick = pick_heads(g)
        gm = gm_ref[:, cols]
        wide = gate_ref[:, cols].astype(F32)
        sig = jax.nn.sigmoid(wide)
        silu = wide * sig
        y = y_ref[:, cols].astype(F32)
        gated = y * silu
        dgain_ref[0:1, cols] += jnp.sum(gm * gated * rms, axis=0, keepdims=True)
        dgated = rms * (gm * gain_ref[:, cols]) - gated * shrink
        dy = dgated * silu
        dy_ref[:, cols] = dy.astype(BF)
        dgate_ref[:, cols] = (dgated * y * (sig * (1.0 + wide - silu))).astype(BF)
        dskip_ref[0:1, cols] += jnp.sum(dy * act_ref[:, cols].astype(F32), axis=0, keepdims=True)
        scaled = (dy * mm(enter2_ref[...], pick)).astype(BF)
        new = mm(turned_ref[pl.ds(STATE, STATE), :], scaled)
        add_ref[0, :, cols] = new.astype(BF)
        acc_ref[:, cols] += gain_row(run_ref[0:1, :], g) * new
    run_ref[0:1, :] += cum_ref[SPAN - 1 : SPAN, :]

    @pl.when(c == pl.num_programs(0) - 1)
    def _():
        first_ref[...] = acc_ref[...].astype(BF)


def conv_back(grad_of, proj_ref, slope_ref, g_ref, taps_ref, masks_ref, rows, dproj_ref, dtaps_ref):
    width = proj_ref.shape[1]
    g_ref[pl.ds(0, HALO), :] = jnp.zeros((HALO, width), F32)
    g_ref[pl.ds(HALO + rows, 8), :] = jnp.zeros((8, width), F32)
    bias = jnp.zeros((8, width), F32)
    for c in range(rows // SPAN):
        at = pl.ds(c * SPAN, SPAN)
        g = grad_of(c) * slope_ref[at, :].astype(F32)
        g_ref[pl.ds(HALO + c * SPAN, SPAN), :] = g
        bias = bias + jnp.sum(g.reshape(SPAN // 8, 8, width), axis=0)
    sums = [jnp.zeros((8, width), F32) for _ in range(KW)]
    pieces = [(0, HALO)] + [(HALO + c * SPAN, SPAN) for c in range(rows // SPAN)]
    for start, size in pieces:
        at = pl.ds(start, size)
        x = proj_ref[at, :].astype(F32)
        total = None
        for k in range(KW):
            g = g_ref[pl.ds(start + KW - 1 - k, size), :]
            if k < KW - 1:
                g = g * masks_ref[at, 4 + k : 5 + k]
            part = taps_ref[k : k + 1, :] * g
            total = part if total is None else total + part
            sums[k] = sums[k] + jnp.sum((g * x).reshape(size // 8, 8, width), axis=0)
        dproj_ref[at, :] = total.astype(BF)
    for k in range(KW):
        dtaps_ref[k : k + 1, :] = jnp.sum(sums[k], axis=0, keepdims=True)
    dtaps_ref[KW : KW + 1, :] = jnp.sum(bias, axis=0, keepdims=True)


def scan_back_kernel(
    base, kq_ref, mixt_ref, step2_ref, enter2_ref, leave2_ref, cum_ref, cumt_ref, act_ref, dy_ref,
    add_ref, radd_ref, into_ref, near_ref, far_ref, run_ref, hp_ref, proj_ref, slope_ref,
    taps_ref, masks_ref,
    dproj_ref, dtaps_ref, dkq_ref, dcum_ref, across_ref, dpre_ref, dstep_ref,
    g_ref, dv_ref, dmix_ref, s_ref,
):
    rows = act_ref.shape[0]
    chunks = rows // SPAN
    local = pl.program_id(0)
    i = local + base
    low = iota((SPAN, 128), 1) < HEAD_DIM
    pick = pick_heads(i)
    seg = sum_heads(i)
    skip = mm(two_parts(jnp.broadcast_to(hp_ref[2:3, :], (16, 128))), pick)[0:1, :]
    select = [
        jnp.where(iota((SPAN, 128), 1) == GROUP * i + h, -1.0, 0.0).astype(BF)
        for h in range(GROUP)
    ]

    @pl.when(local == 0)
    def _():
        dkq_ref[...] = jnp.zeros_like(dkq_ref)
        dcum_ref[...] = jnp.zeros_like(dcum_ref)
        dpre_ref[...] = jnp.zeros_like(dpre_ref)
        dstep_ref[...] = jnp.zeros_like(dstep_ref)
        dmix_ref[...] = jnp.zeros_like(dmix_ref)

    state = into_ref[...]
    gains = []
    for c in range(chunks):
        s_ref[c] = state
        gains.append(gain_row(cum_ref[pl.ds(c * SPAN + SPAN - 1, 1), :], i))
        state = gains[c] * state + add_ref[c].astype(F32)

    later = near_ref[...].astype(F32) + gain_row(run_ref[0:1, :], i) * far_ref[...].astype(F32)
    for c in reversed(range(chunks)):
        at = pl.ds(c * SPAN, SPAN)
        cum = own_lanes(cum_ref[at, :], i)
        enter = mm(enter2_ref[at, :], pick)
        leave = mm(leave2_ref[at, :], pick)
        step_wide = mm(step2_ref[at, :], pick)
        act = act_ref[at, :].astype(F32)
        vdt_f = act * step_wide
        vdt = vdt_f.astype(BF)
        dy = dy_ref[at, :]
        dy_f = dy.astype(F32)
        keys, queries = kq_ref[at, :STATE], kq_ref[at, STATE:]
        here = s_ref[c]
        here_low, later_low = here.astype(BF), later.astype(BF)
        dys = dy_f * enter
        dvdt = leave * mm(keys, later_low)
        sum_out = mm((vdt_f * dvdt).astype(BF), seg)
        turn = mm((dys * mm(queries, here_low)).astype(BF), seg) - sum_out
        dkq_ref[at, STATE:] += mm_nt(dys.astype(BF), here_low)
        dkq_ref[at, :STATE] += mm_nt((vdt_f * leave).astype(BF), later_low)
        both = jnp.sum((here * later).reshape(STATE // 8, 8, WIDE), axis=0)
        both = jnp.sum(both, axis=0, keepdims=True) * gains[c]
        both_high = both.astype(BF)
        both_low = (both - both_high.astype(F32)).astype(BF)
        through = mm(jnp.broadcast_to(both_high, (16, WIDE)), seg)
        through = through + mm(jnp.broadcast_to(both_low, (16, WIDE)), seg)
        inner = []
        dmix = dmix_ref[c]
        for j in range(GROUP // 2):
            pair = vdt[:, 128 * j : 128 * (j + 1)]
            dpair = dy[:, 128 * j : 128 * (j + 1)]
            total = None
            for s in range(2):
                h = 2 * j + s
                gap = cumt_ref[0, h : h + 1, at] - cum[:, h : h + 1]
                decay = jnp.exp(jnp.minimum(gap, 0.0))
                weights = mixt_ref[c] * decay
                dpart = jnp.where(low if s == 0 else ~low, dpair, jnp.zeros_like(dpair))
                dweights = mm_nt(pair, dpart)
                new = mm(weights.astype(BF), dpart)
                total = new if total is None else total + new
                dmix = dmix + dweights * decay
                moved = (dweights * weights).astype(BF)
                turn = turn + mm(moved, select[h])
                across_ref[pl.ds(GROUP * local + h, 1), at] = jnp.sum(
                    moved.astype(F32), axis=0, keepdims=True
                )
            inner.append(total)
        dmix_ref[c] = dmix
        dvdt = dvdt + jnp.concatenate(inner, axis=1)
        dcum_ref[at, :] += turn
        dpre = jnp.sum(sum_out, axis=0, keepdims=True) + through[0:1, :]
        dpre_ref[8 * c : 8 * c + 1, :] += dpre
        dstep_ref[at, :] += mm((act * dvdt).astype(BF), seg)
        dv_ref[at, :] = step_wide * dvdt + skip * dy_f
        later = gains[c] * later + radd_ref[c].astype(F32)

    conv_back(
        lambda c: dv_ref[pl.ds(c * SPAN, SPAN), :], proj_ref, slope_ref, g_ref, taps_ref,
        masks_ref, rows, dproj_ref, dtaps_ref,
    )

    @pl.when(local == pl.num_programs(0) - 1)
    def _():
        for c in range(chunks):
            at = pl.ds(c * SPAN, SPAN)
            dmix = jnp.where(tri(False), dmix_ref[c], 0.0).astype(BF)
            dkq_ref[at, :STATE] += mm(dmix, kq_ref[at, STATE:])
            dkq_ref[at, STATE:] += mm_tn(dmix, kq_ref[at, :STATE])


def last_kernel(*refs):
    parts = [refs[5 * k : 5 * k + 5] for k in range(CALLS)]
    (
        raw_ref, step_ref, hp_ref, proj_ref, slope_ref, taps_ref, masks_ref,
        dproj_ref, dtaps_ref, sums_ref, g_ref,
    ) = refs[5 * CALLS :]
    rows = raw_ref.shape[0]
    upper = jnp.where(tri(False), 1.0, 0.0).astype(F32)
    rate = jnp.exp(hp_ref[1:2, :])
    d_log = jnp.zeros((1, 128), F32)
    d_bias = jnp.zeros((1, 128), F32)
    dproj_ref[pl.ds(0, HALO), pl.ds(WIDE, 128)] = jnp.zeros((HALO, 128), BF)

    def added_up(k, at, cols=slice(None)):
        total = parts[0][k][at, cols]
        for part in parts[1:]:
            total = total + part[k][at, cols]
        return total

    conv_back(
        lambda c: added_up(0, pl.ds(c * SPAN, SPAN)), proj_ref, slope_ref, g_ref, taps_ref,
        masks_ref, rows, dproj_ref.at[:, pl.ds(0, WIDE)], dtaps_ref,
    )
    for c in range(rows // SPAN):
        at = pl.ds(c * SPAN, SPAN)
        across = jnp.concatenate([part[2][:, at] for part in parts], axis=0)
        across = jnp.concatenate([across, jnp.zeros((128 - HEADS, SPAN), F32)], axis=0)
        turn = across.T + added_up(1, at)
        ddecay = jnp.dot(upper, turn, precision=EXACT, preferred_element_type=F32)
        ddecay = ddecay + added_up(3, pl.ds(8 * c, 1))
        step = step_ref[at, :]
        d_log = d_log - jnp.sum(ddecay * step * rate, axis=0, keepdims=True)
        draw = added_up(4, at) - ddecay * rate
        draw = draw * jax.nn.sigmoid(raw_ref[at, :] + hp_ref[0:1, :])
        draw = jnp.where(iota((SPAN, 128), 1) < HEADS, draw, 0.0)
        d_bias = d_bias + jnp.sum(draw, axis=0, keepdims=True)
        dproj_ref[pl.ds(HALO + c * SPAN, SPAN), pl.ds(WIDE, 128)] = draw.astype(BF)
    sums_ref[...] = jnp.zeros_like(sums_ref)
    sums_ref[0:1, :] = d_log
    sums_ref[1:2, :] = d_bias


def tokens_kernel(*refs):
    me_ref, tokens_ref, cot_ref, gain_ref, part_ref = refs[:5]
    dprojs = refs[5 : 5 + CALLS + 1]
    back_ref = refs[6 + CALLS]
    wcs = refs[7 + CALLS : 11 + CALLS]
    dtws = refs[11 + CALLS : 15 + CALLS]
    grad_ref, dgain_ref, gn_ref = refs[15 + CALLS :]
    c = pl.program_id(0)
    me = me_ref[0]
    size, model = tokens_ref.shape
    quarter = model // 4
    start = pl.multiple_of(HALO + c * size, HALO)

    @pl.when(c == 0)
    def _():
        dgain_ref[...] = jnp.zeros_like(dgain_ref)

    width = PER_CALL * WIDE
    for flip in range(4):
        own = pl.ds(pl.multiple_of((me ^ flip) * quarter, quarter), quarter)
        total = part_ref[:, own]
        for k in range(CALLS):
            total = total + mm_nt(
                dprojs[k][pl.ds(start, size), :], wcs[flip][:, pl.ds(k * width, width)]
            )
        total = total + mm_nt(
            dprojs[CALLS][pl.ds(start, size), pl.ds(0, WIDE)], wcs[flip][:, pl.ds(INNER, WIDE)]
        )
        total = total + mm(
            dprojs[CALLS][pl.ds(start, size), pl.ds(WIDE, 128)],
            dtws[flip][pl.ds(0, 128), pl.ds(0, quarter)],
        )
        gn_ref[:, own] = total

    @pl.when(c == pl.num_programs(0) - 1)
    def _():
        for flip in range(4):
            own = pl.ds(pl.multiple_of((me ^ flip) * quarter, quarter), quarter)
            gn_ref[pl.ds(size - HALO, HALO), own] += mm_nt(back_ref[...], wcs[flip][...])

    hidden = tokens_ref[...].astype(F32)
    inv = lax.rsqrt(jnp.mean(hidden * hidden, axis=-1, keepdims=True) + EPSILON)
    gn = gn_ref[...]
    scaled = hidden * inv
    dgain_ref[0:1, :] += jnp.sum(gn * scaled, axis=0, keepdims=True)
    pulled = gn * gain_ref[...]
    mean = jnp.mean(pulled * scaled, axis=-1, keepdims=True)
    grad_ref[...] = cot_ref[...].astype(F32) + inv * (pulled - scaled * mean)


def whole(shape):
    zeros = (0,) * len(shape)
    return pl.BlockSpec(shape, lambda i: zeros)


def scalar():
    return pl.BlockSpec(memory_space=pltpu.SMEM)


def sds(shape, dtype):
    return jax.ShapeDtypeStruct(shape, dtype)


def passed_along(value, steps):
    count = lax.axis_size("shard")
    pairs = [(a, a + steps) for a in range(count) if 0 <= a + steps < count]
    return lax.ppermute(value, "shard", pairs)


def swap(value, axis, bit):
    count = lax.axis_size(axis)
    return lax.ppermute(value, axis, [(a, a ^ bit) for a in range(count)])


def after(value, *others):
    return lax.optimization_barrier((value,) + others)[0]


def gather_pieces(mine):
    across = swap(mine, "shard", 2)
    return mine, swap(mine, "shard", 1), across, swap(across, "shard", 1)


def gather_first(mine, *held_for):
    return mine, swap(mine, "shard", 1), swap(after(mine, *held_for), "shard", 2)


def rep_bits():
    size = lax.axis_size("rep")
    return [1 << b for b in range(size.bit_length() - 1)]


def row_steps(keep, give, scattered):
    keep = lax.optimization_barrier(keep)
    (give,) = yield (give,)
    rows = keep.shape[0] // 2
    chip = keep + swap(give, "shard", 1).astype(F32)
    held, sent = yield (chip[:rows], chip[rows:].astype(BF))
    held = held + swap(sent, "shard", 2).astype(F32)
    rep = lax.axis_index("rep")
    bits = rep_bits()
    for bit in bits[:scattered]:
        at = (rep & bit) // bit
        half = held.shape[0] // 2
        kept = lax.dynamic_slice_in_dim(held, at * half, half, 0)
        sent = lax.dynamic_slice_in_dim(held, (1 - at) * half, half, 0).astype(BF)
        kept, sent = yield (kept, sent)
        held = kept + swap(sent, "rep", bit).astype(F32)
    held = held.astype(BF)
    for bit in bits[scattered:]:
        (held,) = yield (held,)
        held = (held.astype(F32) + swap(held, "rep", bit).astype(F32)).astype(BF)
    for bit in reversed(bits[:scattered]):
        (held,) = yield (held,)
        at = (rep & bit) // bit
        other = swap(held, "rep", bit)
        held = jnp.concatenate(
            [jnp.where(at == 0, held, other), jnp.where(at == 0, other, held)], axis=0
        )
    yield (held,)


class RowSum:
    def __init__(self, keep, give, scattered):
        self.steps = row_steps(keep, give, scattered)
        self.waiting = next(self.steps)

    def take(self, values):
        try:
            self.waiting = self.steps.send(values)
        except StopIteration:
            self.waiting = values

    def result(self):
        for _ in range(16):
            self.take(self.waiting)
        return self.waiting[0].astype(F32)


def ordered(value, *sums):
    out = lax.optimization_barrier((value,) + tuple(one.waiting for one in sums))
    for one, values in zip(sums, out[1:]):
        one.take(values)
    return out[0]


def reduce_small(vector):
    for bit in (1, 2):
        vector = vector + swap(vector, "shard", bit)
    for bit in rep_bits():
        vector = vector + swap(vector, "rep", bit)
    return vector


def on_device(
    tokens, segments, norm_gain, in_weight, dt_weight, conv_weight, conv_bias, dt_bias, a_log,
    d_skip, gate_gain, out_weight, cotangent,
):
    rows, model = tokens.shape
    ext = rows + HALO
    chunks = rows // SPAN
    mine_conv = conv_bias.shape[0]
    conv = 4 * mine_conv
    me = lax.axis_index("shard")
    at_me = me.astype(jnp.int32).reshape(1)

    token_edge = passed_along(tokens[-HALO:], 1)
    prior = passed_along(segments[-8:] + 1, 1) - 1
    docs = jnp.concatenate([jnp.full((16,), -1, jnp.int32), prior, segments, jnp.full((8,), -1, jnp.int32)])
    docs = docs[:, None]

    def line(*parts):
        flat = jnp.concatenate([part.reshape(-1) for part in parts])
        return jnp.pad(flat, (0, mine_conv - flat.shape[0]))[None]

    turned_dt = jnp.pad(dt_weight.T, ((0, 128 - HEADS), (0, mine_conv - dt_weight.shape[0])))
    packed = jnp.concatenate(
        [turned_dt, conv_weight.T, conv_bias[None], line(gate_gain), line(norm_gain),
         line(dt_bias, a_log, d_skip)], axis=0
    )
    packs = gather_pieces(packed)
    across = packs[2]
    own, beside, far, corner = [part[128:] for part in packs]
    core, side = (me & 1) == 0, (me & 2) == 0
    left, right = jnp.where(core, own, beside), jnp.where(core, beside, own)
    up, down = jnp.where(core, far, corner), jnp.where(core, corner, far)
    pieces = [
        jnp.where(side, left, up), jnp.where(side, right, down),
        jnp.where(side, up, left), jnp.where(side, down, right),
    ]
    tables = jnp.stack(pieces).astype(F32)
    taps = jnp.concatenate(pieces, axis=1).astype(F32)
    gate_row = tables[:, 5, : gate_gain.shape[0]].reshape(1, INNER)
    norm_row = tables[:, 6, : norm_gain.shape[0]].reshape(1, model)
    per_head = HEADS // 4
    hp = tables[:, 7, : 3 * per_head].reshape(4, 3, per_head).transpose(1, 0, 2).reshape(3, HEADS)
    hp = jnp.pad(hp, ((0, 5), (0, 128 - HEADS)))
    wc = gather_first(in_weight[:, INNER:], across, token_edge, prior)
    gate_columns = in_weight[:, :INNER]

    half = model // 2
    xk, xg, plain = pl.pallas_call(
        norm_kernel,
        grid=(1,),
        in_specs=[scalar(), whole((HALO, model)), whole((rows, model)), whole((1, model))],
        out_specs=[whole((ext, half)), whole((ext, half)), whole((rows, model))],
        out_shape=[sds((ext, half), BF), sds((ext, half), BF), sds((rows, model), BF)],
        compiler_params=params(),
        cost_estimate=cost(4),
        name="norm_in",
    )(at_me, token_edge, tokens, norm_row)

    taps, hp, gate_columns, xk, xg, plain, wc_far = lax.optimization_barrier(
        (taps, hp, gate_columns, xk, xg, plain, wc[2])
    )
    wc = wc[:2] + (wc_far, swap(wc_far, "shard", 1))
    wg = gather_first(gate_columns, wc_far)
    wide_rows = out_weight.shape[0] // 2
    kq_block = INNER // WIDE
    quarter = model // 4
    whole_x = [whole((ext, half)), whole((ext, half))]
    head_table = whole((rows, 128))
    docs_rows = docs.shape[0]
    proj_kq, kq, slope_kq, turned, raw, step, cum, cumt, mix, mixt, masks, run, step2, enter2, leave2 = pl.pallas_call(
        first_kernel,
        grid=(1,),
        in_specs=whole_x
        + [pl.BlockSpec((quarter, WIDE), lambda i: (0, kq_block))] * 4
        + [whole(packed.shape)] * 4
        + [
            pl.BlockSpec((8, WIDE), lambda i: (0, kq_block)), whole((8, 128)),
            whole((docs_rows, 1)),
        ],
        out_specs=[
            whole((ext, WIDE)), whole((rows, WIDE)), whole((rows, WIDE)), whole((WIDE, rows)),
            head_table, head_table, head_table, whole((GROUPS, GROUP, rows)),
            whole((chunks, SPAN, SPAN)), whole((chunks, SPAN, SPAN)), whole((ext, 8)),
            whole((8, 128)), head_table, head_table, head_table,
        ],
        out_shape=[
            sds((ext, WIDE), BF), sds((rows, WIDE), BF), sds((rows, WIDE), BF),
            sds((WIDE, rows), BF), sds((rows, 128), F32), sds((rows, 128), F32),
            sds((rows, 128), F32), sds((GROUPS, GROUP, rows), F32),
            sds((chunks, SPAN, SPAN), F32), sds((chunks, SPAN, SPAN), F32), sds((ext, 8), F32),
            sds((8, 128), F32), sds((rows, 128), BF), sds((rows, 128), BF), sds((rows, 128), BF),
        ],
        scratch_shapes=[pltpu.VMEM((ext, WIDE), F32)],
        compiler_params=params(),
        cost_estimate=cost(8),
        name="keys_queries",
    )(xk, xg, *wc, *packs, taps, hp, docs)

    def columns(height, base=0):
        return pl.BlockSpec((height, WIDE), lambda i: (0, i + base))

    def states(base=0):
        return pl.BlockSpec((chunks, STATE, WIDE), lambda i: (0, 0, i + base))

    def cumt_spec(base=0):
        return pl.BlockSpec((1, GROUP, rows), lambda i: (i + base, 0, 0))

    wo_a = gather_first(out_weight[:wide_rows], run)
    proj_v, act, slope_v, adds, last = pl.pallas_call(
        state_kernel,
        grid=(GROUPS,),
        in_specs=whole_x + [columns(quarter)] * 4 + [
            columns(8), whole((ext, 8)), head_table, head_table, head_table, whole((WIDE, rows)),
        ],
        out_specs=[columns(ext), columns(rows), columns(rows), states(), columns(STATE)],
        out_shape=[
            sds((ext, INNER), BF), sds((rows, INNER), BF), sds((rows, INNER), BF),
            sds((chunks, STATE, INNER), BF), sds((STATE, INNER), BF),
        ],
        scratch_shapes=[pltpu.VMEM((ext, WIDE), F32)],
        compiler_params=params(),
        cost_estimate=cost(20),
        name="values_states",
    )(xk, xg, *wc, taps, masks, step2, leave2, cum, turned)

    wg_far, wo_far, last, act, adds, proj_v, slope_v = lax.optimization_barrier(
        (wg[2], wo_a[2], last, act, adds, proj_v, slope_v)
    )
    wg = wg[:2] + (wg_far, swap(wg_far, "shard", 1))
    wo_a = wo_a[:2] + (wo_far, swap(wo_far, "shard", 1))
    run_prev, run_next = passed_along(run, 1), passed_along(run, -1)
    near, far = passed_along(last, 1), passed_along(last, 2)

    inside, gate = pl.pallas_call(
        inside_kernel,
        grid=(GROUPS,),
        in_specs=whole_x + [columns(quarter)] * 4 + [
            columns(rows), head_table, head_table, cumt_spec(), whole((chunks, SPAN, SPAN)),
            whole((8, 128)),
        ],
        out_specs=[columns(rows), columns(rows)],
        out_shape=[sds((rows, INNER), F32), sds((rows, INNER), BF)],
        compiler_params=params(),
        cost_estimate=cost(20),
        name="scan_inside",
    )(xk, xg, *wg, act, step2, cum, cumt, mix, hp)

    near, far, run_prev, inside, gate = lax.optimization_barrier(
        (near, far, run_prev, inside, gate)
    )
    wo_b = gather_first(out_weight[wide_rows:], near)
    y, mixed, rms, into = pl.pallas_call(
        mixed_kernel,
        grid=(GROUPS,),
        in_specs=[
            columns(rows), columns(rows), whole((rows, WIDE)), head_table, head_table, states(),
            columns(STATE), columns(STATE), whole((8, 128)), whole((1, INNER)),
        ],
        out_specs=[columns(rows), whole((rows, INNER)), head_table, columns(STATE)],
        out_shape=[
            sds((rows, INNER), BF), sds((rows, INNER), BF), sds((rows, 128), F32),
            sds((STATE, INNER), F32),
        ],
        scratch_shapes=[
            pltpu.VMEM((GROUPS, rows, WIDE), F32), pltpu.VMEM((rows, 128), F32),
        ],
        compiler_params=params(),
        cost_estimate=cost(10),
        name="scan_gate",
    )(inside, gate, kq, enter2, cum, adds, near, far, run_prev, gate_row)
    wo_far, y, mixed, rms, into = lax.optimization_barrier((wo_b[2], y, mixed, rms, into))
    wo_b = wo_b[:2] + (wo_far, swap(wo_far, "shard", 1))
    wo = [part for both in zip(wo_a, wo_b) for part in both]

    def by_chunk(width):
        return pl.BlockSpec((SPAN, width), lambda c: (c, 0))

    grad_out = mm_tn(mixed, cotangent).astype(BF)
    grad_out, cum_then = lax.optimization_barrier((grad_out, cum))
    sum_out = lax.psum_scatter(grad_out, "shard", scatter_dimension=0, tiled=True)
    wo_specs = [whole((wide_rows, model))] * 8

    dy, dgate, dgain, dskip, radds, first = pl.pallas_call(
        gate_back_kernel,
        grid=(chunks,),
        in_specs=[scalar(), by_chunk(model)] + wo_specs + [
            by_chunk(INNER), by_chunk(INNER), by_chunk(128), whole((1, INNER)), by_chunk(INNER),
            pl.BlockSpec((WIDE, SPAN), lambda c: (0, c)), by_chunk(128), by_chunk(128),
        ],
        out_specs=[
            by_chunk(INNER), by_chunk(INNER), whole((8, INNER)), whole((8, INNER)),
            pl.BlockSpec((1, STATE, INNER), lambda c: (c, 0, 0)), whole((STATE, INNER)),
        ],
        out_shape=[
            sds((rows, INNER), BF), sds((rows, INNER), BF), sds((8, INNER), F32),
            sds((8, INNER), F32), sds((chunks, STATE, INNER), BF), sds((STATE, INNER), BF),
        ],
        scratch_shapes=[
            pltpu.VMEM((SPAN, INNER), F32), pltpu.VMEM((8, 128), F32),
            pltpu.VMEM((STATE, INNER), F32),
        ],
        compiler_params=params(),
        cost_estimate=cost(22),
        name="gate_back",
    )(at_me, cotangent, *wo, y, gate, rms, gate_row, act, turned, enter2, cum_then)

    grad_gate = mm_tn(plain, dgate).astype(BF)
    near, far = passed_along(first, -1), passed_along(first, -2)
    grad_gate, mixed_then = lax.optimization_barrier((grad_gate, mixed))
    sum_gate = lax.psum_scatter(grad_gate, "shard", scatter_dimension=0, tiled=True)
    output, part = pl.pallas_call(
        rows_kernel,
        grid=(chunks,),
        in_specs=[scalar(), by_chunk(INNER), by_chunk(model), by_chunk(INNER)] + wo_specs
        + [whole((quarter, INNER))] * 4,
        out_specs=[by_chunk(model), by_chunk(model)],
        out_shape=[sds((rows, model), BF), sds((rows, model), F32)],
        compiler_params=params(),
        cost_estimate=cost(18),
        name="rows_out",
    )(at_me, mixed_then, tokens, dgate, *wo, *wg)
    near, far, output, part, run_next = lax.optimization_barrier((near, far, output, part, run_next))

    dprojs, dtaps, partials = [], [], []
    width = PER_CALL * WIDE
    sums = []

    def add_sum(parts, scattered):
        grad = parts[0] if len(parts) == 1 else jnp.concatenate(parts, axis=1)
        sums.append(RowSum(mm_tn(xk, grad), mm_tn(xg, grad).astype(BF), scattered))

    cum_then, output = lax.optimization_barrier((cum, output))
    for k in range(CALLS):
        base = PER_CALL * k
        dproj, dtap, *rest = pl.pallas_call(
            partial(scan_back_kernel, base),
            grid=(PER_CALL,),
            in_specs=[
                whole((rows, WIDE)), whole((chunks, SPAN, SPAN)), head_table, head_table,
                head_table, head_table, cumt_spec(base), columns(rows, base), columns(rows, base),
                states(base), states(base), columns(STATE, base), columns(STATE, base),
                columns(STATE, base), whole((8, 128)), whole((8, 128)), columns(ext, base),
                columns(rows, base), columns(8, base), whole((ext, 8)),
            ],
            out_specs=[
                columns(ext), columns(8), whole((rows, WIDE)), head_table,
                whole((GROUP * PER_CALL, rows)), whole((8 * chunks, 128)), head_table,
            ],
            out_shape=[
                sds((ext, width), BF), sds((8, width), F32), sds((rows, WIDE), F32),
                sds((rows, 128), F32), sds((GROUP * PER_CALL, rows), F32),
                sds((8 * chunks, 128), F32), sds((rows, 128), F32),
            ],
            scratch_shapes=[
                pltpu.VMEM((ext + 8, WIDE), F32), pltpu.VMEM((rows, WIDE), F32),
                pltpu.VMEM((chunks, SPAN, SPAN), F32), pltpu.VMEM((chunks, STATE, WIDE), F32),
            ],
            compiler_params=params(),
            cost_estimate=cost(15),
            name="scan_back",
        )(kq, mixt, step2, enter2, leave2, cum_then, cumt, act, dy, adds, radds, into, near, far,
          run_next, hp, proj_v, slope_v, taps, masks)
        if k == 0:
            sum_out, dproj = lax.optimization_barrier((sum_out, dproj))
            sum_out = lax.psum(sum_out, "rep")
        elif k == 1:
            sum_gate, dproj = lax.optimization_barrier((sum_gate, dproj))
            sum_gate = lax.psum(sum_gate, "rep")
        dproj, dtap, rest = ordered((dproj, dtap, rest), *sums)
        dprojs.append(dproj)
        dtaps.append(dtap)
        partials.extend(rest)
        if k == 1:
            add_sum(dprojs, 2)
        elif k > 1:
            add_sum([dproj], 1)
        cum_then = ordered(cum, *sums[-1:])

    raw_then, cum_then = lax.optimization_barrier((raw, cum_then))
    tail = WIDE + 128
    dlast, dtap, head_sums = pl.pallas_call(
        last_kernel,
        grid=(1,),
        in_specs=[
            whole((rows, WIDE)), head_table, whole((GROUP * PER_CALL, rows)),
            whole((8 * chunks, 128)), head_table,
        ] * CALLS + [
            head_table, head_table, whole((8, 128)), whole((ext, WIDE)), whole((rows, WIDE)),
            pl.BlockSpec((8, WIDE), lambda i: (0, kq_block)), whole((ext, 8)),
        ],
        out_specs=[whole((ext, tail)), whole((8, WIDE)), whole((8, 128))],
        out_shape=[sds((ext, tail), BF), sds((8, WIDE), F32), sds((8, 128), F32)],
        scratch_shapes=[pltpu.VMEM((ext + 8, WIDE), F32)],
        compiler_params=params(),
        cost_estimate=cost(8),
        name="last_back",
    )(*partials, raw_then, step, hp, proj_kq, slope_kq, taps, masks)
    dlast, dtap, head_sums = ordered((dlast, dtap, head_sums), *sums)
    dprojs.append(dlast)
    dtaps.append(dtap)

    add_sum(dprojs[CALLS:], 0)
    part = ordered(part, sums[3])
    heads = jnp.concatenate([part[:HALO] for part in dprojs[:CALLS]] + [dlast[:HALO, :WIDE]], axis=1)
    back = passed_along(heads, -1)
    grad_tokens, g_norm = pl.pallas_call(
        tokens_kernel,
        grid=(chunks,),
        in_specs=[scalar(), by_chunk(model), by_chunk(model), whole((1, model)), by_chunk(model)]
        + [whole((ext, width))] * CALLS
        + [whole((ext, tail)), whole((HALO, conv))]
        + [whole((quarter, conv))] * 4
        + [whole(packed.shape)] * 4,
        out_specs=[by_chunk(model), whole((8, model))],
        out_shape=[sds((rows, model), F32), sds((8, model), F32)],
        scratch_shapes=[pltpu.VMEM((SPAN, model), F32)],
        compiler_params=params(),
        cost_estimate=cost(18),
        name="tokens_back",
    )(at_me, tokens, cotangent, norm_row, part, *dprojs, back, *wc, *packs)

    grad_tokens, g_norm = ordered((grad_tokens, g_norm), *sums)
    dtaps = jnp.concatenate(dtaps, axis=1)
    g_skip = jnp.sum(dskip[0].reshape(HEADS, HEAD_DIM), axis=1)
    parts = (
        g_norm[0], dtaps[:KW].T.reshape(-1), dtaps[KW], head_sums[1, :HEADS],
        head_sums[0, :HEADS], g_skip, dgain[0],
    )
    total = reduce_small(jnp.concatenate(parts))
    outs, start = [], 0
    for part in parts:
        size = part.shape[0] // 4
        outs.append(lax.dynamic_slice(total, (start + me * size,), (size,)))
        start += part.shape[0]
    s_norm, s_conv, s_cbias, s_step, s_decay, s_skip, s_gate = outs
    sums = [one.result() for one in sums]
    s_in = jnp.concatenate([sum_gate.astype(F32)] + sums[:3] + [sums[3][:, :WIDE]], axis=1)
    s_dt = sums[3][:, WIDE : WIDE + HEADS]
    return (
        output, grad_tokens, s_norm, s_in, s_dt, s_conv.reshape(-1, KW), s_cbias, s_step, s_decay,
        s_skip, s_gate, sum_out.astype(F32),
    )


def solution(mesh):
    spread = P(("rep", "shard"), None)
    row = P("shard")
    table = P("shard", None)
    return jax.shard_map(
        on_device,
        mesh=mesh,
        in_specs=(
            spread, P(("rep", "shard")), row, table, table, table, row, row, row, row, row, table,
            spread,
        ),
        out_specs=(
            spread, spread, row, table, table, table, row, row, row, row, row, table,
        ),
        check_vma=False,
    )
```

```python
from functools import partial

import jax
import jax.numpy as jnp
from jax import lax
from jax.experimental import pallas as pl
from jax.experimental.pallas import tpu as pltpu
from jax.sharding import PartitionSpec as P

HEADS = 32
HEAD_DIM = 64
STATE = 128
KW = 4
SPAN = 256
INNER = 2048
GROUP = 4
WIDE = GROUP * HEAD_DIM
GROUPS = HEADS // GROUP
ORDER = (0, 2, 1, 3)
CALLS = (4, 2, 2)
HALO = 16
CUT = -200.0
EPSILON = 1e-05
EXACT = lax.Precision.HIGHEST
BF = jnp.bfloat16
F32 = jnp.float32
VMEM = 56 * 1024 * 1024


def params():
    return pltpu.CompilerParams(vmem_limit_bytes=VMEM)


def cost(micros):
    return pl.CostEstimate(flops=int(micros * 2.0e7), bytes_accessed=0, transcendentals=0)


def mm(a, b):
    return jnp.dot(a, b, preferred_element_type=F32)


def mm_nt(a, b):
    return lax.dot_general(a, b, (((1,), (1,)), ((), ())), preferred_element_type=F32)


def mm_tn(a, b):
    return lax.dot_general(a, b, (((0,), (0,)), ((), ())), preferred_element_type=F32)


def iota(shape, dim):
    return lax.broadcasted_iota(jnp.int32, shape, dim)


def own_lanes(full, step):
    return pltpu.roll(full, lax.rem(128 - GROUP * step, 128), 1)


def pick_heads(step):
    row, col = iota((128, WIDE), 0), iota((128, WIDE), 1)
    wanted = GROUP * step + col // HEAD_DIM
    return jnp.where((row == wanted) | (row == wanted + HEADS), 1.0, 0.0).astype(BF)


def sum_heads(step):
    row, col = iota((WIDE, 128), 0), iota((WIDE, 128), 1)
    return jnp.where(GROUP * step + row // HEAD_DIM == col, 1.0, 0.0).astype(BF)


def two_parts(value):
    value = jnp.where(iota(value.shape, 1) < HEADS, value, 0.0)
    high = value.astype(BF).astype(F32)
    return (high + pltpu.roll(value - high, HEADS, 1)).astype(BF)


def tri(lower):
    a, b = iota((SPAN, SPAN), 0), iota((SPAN, SPAN), 1)
    return (a >= b) if lower else (a <= b)


def norm_kernel(me_ref, edge_ref, tokens_ref, gain_ref, keep_ref, give_ref, plain_ref):
    rows, model = tokens_ref.shape
    quarter = model // 4
    me = me_ref[0]

    def one(ref, start, size, out):
        hidden = ref[pl.ds(start, size), :].astype(F32)
        inv = lax.rsqrt(jnp.mean(hidden * hidden, axis=-1, keepdims=True) + EPSILON)
        for place, flip in enumerate(ORDER):
            at = pl.ds(pl.multiple_of((me ^ flip) * quarter, quarter), quarter)
            part = ref[pl.ds(start, size), at].astype(F32) * inv * gain_ref[:, at]
            target = keep_ref if place < 2 else give_ref
            cols = pl.ds((place % 2) * quarter, quarter)
            target[pl.ds(out, size), cols] = part.astype(BF)
            if out >= HALO:
                plain_ref[pl.ds(start, size), at] = part.astype(BF)

    one(edge_ref, 0, HALO, 0)
    for c in range(rows // SPAN):
        one(tokens_ref, c * SPAN, SPAN, HALO + c * SPAN)


def project(xk_ref, xg_ref, w_refs, start, size):
    quarter = xk_ref.shape[1] // 2
    at = pl.ds(start, size)
    total = None
    for place, flip in enumerate(ORDER):
        x_ref = xk_ref if place < 2 else xg_ref
        part = mm(x_ref[at, pl.ds((place % 2) * quarter, quarter)], w_refs[flip][...])
        total = part if total is None else total + part
    return total


def conv_rows(p_ref, taps_ref, masks, c):
    total = jnp.broadcast_to(taps_ref[KW : KW + 1, :], (SPAN, p_ref.shape[1]))
    base = HALO - KW + 1 + c * SPAN
    for k in range(KW):
        part = taps_ref[k : k + 1, :] * p_ref[pl.ds(base + k, SPAN), :]
        if k < KW - 1:
            part = part * masks[:, k : k + 1]
        total = total + part
    return total


def project_conv(xk_ref, xg_ref, w_refs, taps_ref, masks_ref, proj_ref, act_ref, slope_ref, p_ref, c):
    at = pl.ds(c * SPAN, SPAN)
    up = pl.ds(HALO + c * SPAN, SPAN)
    if c == 0:
        edge = project(xk_ref, xg_ref, w_refs, 0, HALO).astype(BF)
        proj_ref[pl.ds(0, HALO), :] = edge
        p_ref[pl.ds(0, HALO), :] = edge.astype(F32)
    for d in (0, 1) if c == 0 else (c + 1,):
        if d * SPAN < act_ref.shape[0]:
            ahead = pl.ds(HALO + d * SPAN, SPAN)
            own = project(xk_ref, xg_ref, w_refs, HALO + d * SPAN, SPAN).astype(BF)
            proj_ref[ahead, :] = own
            p_ref[ahead, :] = own.astype(F32)
    cs = conv_rows(p_ref, taps_ref, masks_ref[up, :], c)
    sig = jax.nn.sigmoid(cs)
    act = cs * sig
    act_ref[at, :] = act.astype(BF)
    slope_ref[at, :] = (sig * (1.0 + cs - act)).astype(BF)
    return act


def first_kernel(
    xk_ref, xg_ref, w0, w1, w2, w3, d0, d1, d2, d3, taps_ref, hp_ref, line_ref,
    proj_ref, act_ref, slope_ref, turned_ref, raw_ref, step_ref, cum_ref, cumt_ref, mix_ref,
    mixt_ref, masks_ref, run_ref, step2_ref, enter2_ref, leave2_ref, give2_ref, p_ref, docs_ref,
):
    rows = act_ref.shape[0]
    ext = rows + HALO
    lower = tri(True)
    ones_lower = jnp.where(lower, 1.0, 0.0).astype(F32)
    for b in range(line_ref.shape[1] // 128):
        block = jnp.broadcast_to(line_ref[0:1, pl.ds(128 * b, 128)], (128, 128))
        docs_ref[pl.ds(128 * b, 128), :] = block.T[:, 0:1]
    here = docs_ref[pl.ds(8, ext), :]
    lane = iota((ext, 8), 1)
    inside = iota((ext, 1), 0) - HALO
    masks = jnp.zeros((ext, 8), F32)
    for k in range(KW - 1):
        back = docs_ref[pl.ds(8 - KW + 1 + k, ext), :] == here
        masks = masks + jnp.where((lane == k) & back, 1.0, 0.0)
        ahead = (docs_ref[pl.ds(8 + KW - 1 - k, ext), :] == here) & (inside + KW - 1 - k >= 0)
        masks = masks + jnp.where((lane == 4 + k) & ahead, 1.0, 0.0)
    masks_ref[...] = masks
    total = jnp.zeros((1, 128), F32)
    for c in range(rows // SPAN):
        at = pl.ds(c * SPAN, SPAN)
        up = pl.ds(HALO + c * SPAN, SPAN)
        act = project_conv(
            xk_ref, xg_ref, (w0, w1, w2, w3), taps_ref, masks_ref, proj_ref, act_ref, slope_ref,
            p_ref, c,
        )
        turned_ref[:, at] = act.T.astype(BF)
        act = act.astype(BF)
        keys, queries = act[:, :STATE], act[:, STATE:]
        mix_ref[c] = jnp.where(lower, mm_nt(queries, keys), 0.0)
        mixt_ref[c] = jnp.where(tri(False), mm_nt(keys, queries), 0.0)
        quarter = xk_ref.shape[1] // 2
        raw = jnp.zeros((SPAN, 128), F32)
        for place, flip in enumerate(ORDER):
            x_ref = xk_ref if place < 2 else xg_ref
            part = x_ref[up, pl.ds((place % 2) * quarter, quarter)]
            raw = raw + mm_nt(part, (d0, d1, d2, d3)[flip][pl.ds(0, 128), pl.ds(0, quarter)])
        raw_ref[at, :] = raw
        step = jax.nn.softplus(raw + hp_ref[0:1, :])
        step_ref[at, :] = step
        cut = 1.0 - masks_ref[up, KW - 2 : KW - 1]
        decays = -step * jnp.exp(hp_ref[1:2, :]) + CUT * cut
        cum = jnp.dot(ones_lower, decays, precision=EXACT, preferred_element_type=F32)
        cum_ref[at, :] = cum
        cumt = lax.dot_general(
            decays, ones_lower, (((0,), (1,)), ((), ())), precision=EXACT,
            preferred_element_type=F32,
        )
        for g in range(GROUPS):
            cumt_ref[g, :, at] = cumt[GROUP * g : GROUP * (g + 1), :]
        end = cum[SPAN - 1 : SPAN, :]
        total = total + end
        step2_ref[at, :] = two_parts(step)
        enter2_ref[at, :] = two_parts(jnp.exp(cum))
        leave = jnp.exp(end - cum)
        leave2_ref[at, :] = two_parts(leave)
        give2_ref[at, :] = two_parts(leave * step)
    run_ref[...] = jnp.broadcast_to(total, (8, 128))


def gain_row(cum_row, step):
    return mm(two_parts(jnp.exp(jnp.broadcast_to(cum_row, (16, 128)))), pick_heads(step))[0:1, :]


def state_kernel(
    xk_ref, xg_ref, w0, w1, w2, w3, taps_ref, masks_ref, give2_ref, cum_ref, turned_ref,
    proj_ref, act_ref, slope_ref, add_ref, last_ref, p_ref,
):
    rows = act_ref.shape[0]
    i = pl.program_id(0)
    pick = pick_heads(i)
    state = jnp.zeros((STATE, WIDE), F32)
    for c in range(rows // SPAN):
        at = pl.ds(c * SPAN, SPAN)
        act = project_conv(
            xk_ref, xg_ref, (w0, w1, w2, w3), taps_ref, masks_ref, proj_ref, act_ref, slope_ref,
            p_ref, c,
        )
        scale = mm(give2_ref[at, :], pick)
        new = mm(turned_ref[pl.ds(0, STATE), at], (act * scale).astype(BF))
        add_ref[c] = new.astype(BF)
        end = cum_ref[pl.ds(c * SPAN + SPAN - 1, 1), :]
        state = gain_row(end, i) * state + new
    last_ref[...] = state.astype(BF)


def inside_kernel(
    xk_ref, xg_ref, w0, w1, w2, w3, act_ref, step2_ref, cum_ref, cumt_ref, mix_ref, hp_ref,
    y_ref, gate_ref,
):
    rows = act_ref.shape[0]
    i = pl.program_id(0)
    low = iota((SPAN, 128), 1) < HEAD_DIM
    pick = pick_heads(i)
    skip = mm(two_parts(jnp.broadcast_to(hp_ref[2:3, :], (16, 128))), pick)[0:1, :]
    for c in range(rows // SPAN):
        at = pl.ds(c * SPAN, SPAN)
        gate_ref[at, :] = project(
            xk_ref, xg_ref, (w0, w1, w2, w3), HALO + c * SPAN, SPAN
        ).astype(BF)
        cum = own_lanes(cum_ref[at, :], i)
        act = act_ref[at, :].astype(F32)
        vdt = (act * mm(step2_ref[at, :], pick)).astype(BF)
        for j in range(GROUP // 2):
            cols = slice(128 * j, 128 * (j + 1))
            pair = vdt[:, cols]
            total = skip[:, cols] * act[:, cols]
            for s in range(2):
                h = 2 * j + s
                gap = cum[:, h : h + 1] - cumt_ref[0, h : h + 1, at]
                weights = (mix_ref[c] * jnp.exp(jnp.minimum(gap, 0.0))).astype(BF)
                part = jnp.where(low if s == 0 else ~low, pair, jnp.zeros_like(pair))
                total = total + mm(weights, part)
            y_ref[at, pl.ds(128 * j, 128)] = total


def mixed_kernel(
    inside_ref, gate_ref, kq_ref, enter2_ref, cum_ref, add_ref, near_ref, far_ref, run_ref,
    gain_ref,
    y_ref, mixed_ref, rms_ref, into_ref, gated_ref, sum_ref,
):
    rows = inside_ref.shape[0]
    i = pl.program_id(0)
    pick = pick_heads(i)
    state = near_ref[...].astype(F32) + gain_row(run_ref[0:1, :], i) * far_ref[...].astype(F32)
    into_ref[...] = state

    @pl.when(i == 0)
    def _():
        sum_ref[...] = jnp.zeros_like(sum_ref)

    for c in range(rows // SPAN):
        at = pl.ds(c * SPAN, SPAN)
        y = mm(enter2_ref[at, :], pick) * mm(kq_ref[at, STATE:], state.astype(BF))
        y = y + inside_ref[at, :]
        y_ref[at, :] = y.astype(BF)
        wide = gate_ref[at, :].astype(F32)
        gated = y * (wide * jax.nn.sigmoid(wide))
        gated_ref[i, at, :] = gated
        squares = gated * gated
        sum_ref[at, :] += squares[:, :128] + squares[:, 128:]
        state = gain_row(cum_ref[pl.ds(c * SPAN + SPAN - 1, 1), :], i) * state + add_ref[c].astype(F32)

    @pl.when(i == GROUPS - 1)
    def _():
        for c in range(rows // SPAN):
            at = pl.ds(c * SPAN, SPAN)
            mean = jnp.sum(sum_ref[at, :], axis=1, keepdims=True) * (1.0 / INNER)
            rms = lax.rsqrt(mean + EPSILON)
            rms_ref[at, :] = jnp.broadcast_to(rms, (SPAN, 128))
            for g in range(GROUPS):
                cols = pl.ds(g * WIDE, WIDE)
                mixed_ref[at, cols] = (gated_ref[g, at, :] * rms * gain_ref[:, cols]).astype(BF)


def rows_kernel(me_ref, mixed_ref, tokens_ref, dgate_ref, *refs):
    wos, wgs = refs[:8], refs[8:12]
    out_ref, part_ref = refs[12:]
    me = me_ref[0]
    per = GROUPS // 4
    quarter = wgs[0].shape[0]
    total = tokens_ref[...].astype(F32)
    for flip in range(4):
        for s in range(per):
            cols = pl.ds(pl.multiple_of(((me ^ flip) * per + s) * WIDE, WIDE), WIDE)
            total = total + mm(mixed_ref[:, cols], wos[per * flip + s][...])
    out_ref[...] = total.astype(BF)
    for flip in range(4):
        own = pl.ds(pl.multiple_of((me ^ flip) * quarter, quarter), quarter)
        part_ref[:, own] = mm_nt(dgate_ref[...], wgs[flip][...])


def gate_back_kernel(
    me_ref, cot_ref, w0, w1, w2, w3, w4, w5, w6, w7, y_ref, gate_ref, rms_ref, gain_ref, act_ref,
    turned_ref, enter2_ref, cum_ref,
    dy_ref, dgate_ref, dgain_ref, dskip_ref, add_ref, first_ref, gm_ref, run_ref, acc_ref,
):
    c = pl.program_id(0)
    me = me_ref[0]

    @pl.when(c == 0)
    def _():
        dgain_ref[...] = jnp.zeros_like(dgain_ref)
        dskip_ref[...] = jnp.zeros_like(dskip_ref)
        acc_ref[...] = jnp.zeros_like(acc_ref)
        run_ref[...] = jnp.zeros_like(run_ref)

    rms = rms_ref[:, 0:1]
    total = jnp.zeros((SPAN, 128), F32)
    cot = cot_ref[...]
    per = GROUPS // 4
    ws = (w0, w1, w2, w3, w4, w5, w6, w7)
    following = mm_nt(cot, ws[0][...])
    for flip in range(4):
        for s in range(per):
            cols = pl.ds(pl.multiple_of(((me ^ flip) * per + s) * WIDE, WIDE), WIDE)
            gm = following
            if per * flip + s + 1 < GROUPS:
                following = mm_nt(cot, ws[per * flip + s + 1][...])
            gm_ref[:, cols] = gm
            wide = gate_ref[:, cols].astype(F32)
            gated = y_ref[:, cols].astype(F32) * (wide * jax.nn.sigmoid(wide))
            q = gm * gain_ref[:, cols] * gated
            total = total + q[:, :128] + q[:, 128:]
    mean = jnp.sum(total, axis=1, keepdims=True) * (1.0 / INNER)
    shrink = rms * rms * rms * mean
    following = mm(enter2_ref[...], pick_heads(0))
    for g in range(GROUPS):
        cols = pl.ds(g * WIDE, WIDE)
        enter = following
        if g + 1 < GROUPS:
            following = mm(enter2_ref[...], pick_heads(g + 1))
        gm = gm_ref[:, cols]
        wide = gate_ref[:, cols].astype(F32)
        sig = jax.nn.sigmoid(wide)
        silu = wide * sig
        y = y_ref[:, cols].astype(F32)
        gated = y * silu
        dgain_ref[0:1, cols] += jnp.sum(gm * gated * rms, axis=0, keepdims=True)
        dgated = rms * (gm * gain_ref[:, cols]) - gated * shrink
        dy = dgated * silu
        dy_ref[:, cols] = dy.astype(BF)
        dgate_ref[:, cols] = (dgated * y * (sig * (1.0 + wide - silu))).astype(BF)
        dskip_ref[0:1, cols] += jnp.sum(dy * act_ref[:, cols].astype(F32), axis=0, keepdims=True)
        scaled = (dy * enter).astype(BF)
        new = mm(turned_ref[pl.ds(STATE, STATE), :], scaled)
        add_ref[0, :, cols] = new.astype(BF)
        acc_ref[:, cols] += gain_row(run_ref[0:1, :], g) * new
    run_ref[0:1, :] += cum_ref[SPAN - 1 : SPAN, :]

    @pl.when(c == pl.num_programs(0) - 1)
    def _():
        first_ref[...] = acc_ref[...].astype(BF)


class ConvBack:
    def __init__(self, proj_ref, slope_ref, g_ref, taps_ref, masks_ref, dproj_ref):
        self.refs = proj_ref, slope_ref, g_ref, taps_ref, masks_ref, dproj_ref
        self.rows, self.width = slope_ref.shape
        g_ref[pl.ds(0, HALO), :] = jnp.zeros((HALO, self.width), F32)
        g_ref[pl.ds(HALO + self.rows, 8), :] = jnp.zeros((8, self.width), F32)
        self.bias = jnp.zeros((8, self.width), F32)
        self.sums = [jnp.zeros((8, self.width), F32) for _ in range(KW)]

    def put(self, c, grad):
        _, slope_ref, g_ref, *_ = self.refs
        g = grad * slope_ref[pl.ds(c * SPAN, SPAN), :].astype(F32)
        g_ref[pl.ds(HALO + c * SPAN, SPAN), :] = g
        self.bias = self.bias + jnp.sum(g.reshape(SPAN // 8, 8, self.width), axis=0)

    def chunk(self, c):
        self.piece(HALO + c * SPAN, SPAN)

    def piece(self, start, size):
        proj_ref, _, g_ref, taps_ref, masks_ref, dproj_ref = self.refs
        at = pl.ds(start, size)
        x = proj_ref[at, :].astype(F32)
        total = None
        for k in range(KW):
            g = g_ref[pl.ds(start + KW - 1 - k, size), :]
            if k < KW - 1:
                g = g * masks_ref[at, 4 + k : 5 + k]
            part = taps_ref[k : k + 1, :] * g
            total = part if total is None else total + part
            self.sums[k] = self.sums[k] + jnp.sum((g * x).reshape(size // 8, 8, self.width), axis=0)
        dproj_ref[at, :] = total.astype(BF)

    def finish(self, dtaps_ref):
        self.piece(0, HALO)
        for k in range(KW):
            dtaps_ref[k : k + 1, :] = jnp.sum(self.sums[k], axis=0, keepdims=True)
        dtaps_ref[KW : KW + 1, :] = jnp.sum(self.bias, axis=0, keepdims=True)


def scan_back_kernel(
    base, kq_ref, mixt_ref, step2_ref, enter2_ref, leave2_ref, cum_ref, cumt_ref, act_ref, dy_ref,
    add_ref, radd_ref, into_ref, near_ref, far_ref, run_ref, hp_ref, proj_ref, slope_ref,
    taps_ref, masks_ref,
    dproj_ref, dtaps_ref, dkq_ref, dcum_ref, across_ref, dpre_ref, dstep_ref,
    g_ref, dmix_ref, s_ref,
):
    rows = act_ref.shape[0]
    chunks = rows // SPAN
    local = pl.program_id(0)
    i = local + base
    low = iota((SPAN, 128), 1) < HEAD_DIM
    pick = pick_heads(i)
    seg = sum_heads(i)
    skip = mm(two_parts(jnp.broadcast_to(hp_ref[2:3, :], (16, 128))), pick)[0:1, :]
    select = [
        jnp.where(iota((SPAN, 128), 1) == GROUP * i + h, -1.0, 0.0).astype(BF)
        for h in range(GROUP)
    ]

    @pl.when(local == 0)
    def _():
        dkq_ref[...] = jnp.zeros_like(dkq_ref)
        dcum_ref[...] = jnp.zeros_like(dcum_ref)
        dpre_ref[...] = jnp.zeros_like(dpre_ref)
        dstep_ref[...] = jnp.zeros_like(dstep_ref)
        dmix_ref[...] = jnp.zeros_like(dmix_ref)

    state = into_ref[...]
    gains = []
    for c in range(chunks):
        s_ref[c] = state
        gains.append(gain_row(cum_ref[pl.ds(c * SPAN + SPAN - 1, 1), :], i))
        state = gains[c] * state + add_ref[c].astype(F32)

    conv = ConvBack(proj_ref, slope_ref, g_ref, taps_ref, masks_ref, dproj_ref)
    later = near_ref[...].astype(F32) + gain_row(run_ref[0:1, :], i) * far_ref[...].astype(F32)
    for c in reversed(range(chunks)):
        at = pl.ds(c * SPAN, SPAN)
        cum = own_lanes(cum_ref[at, :], i)
        enter = mm(enter2_ref[at, :], pick)
        leave = mm(leave2_ref[at, :], pick)
        step_wide = mm(step2_ref[at, :], pick)
        act = act_ref[at, :].astype(F32)
        vdt_f = act * step_wide
        vdt = vdt_f.astype(BF)
        dy = dy_ref[at, :]
        dy_f = dy.astype(F32)
        keys, queries = kq_ref[at, :STATE], kq_ref[at, STATE:]
        here = s_ref[c]
        here_low, later_low = here.astype(BF), later.astype(BF)
        dys = dy_f * enter
        dvdt = leave * mm(keys, later_low)
        sum_out = mm((vdt_f * dvdt).astype(BF), seg)
        turn = mm((dys * mm(queries, here_low)).astype(BF), seg) - sum_out
        dkq_ref[at, STATE:] += mm_nt(dys.astype(BF), here_low)
        dkq_ref[at, :STATE] += mm_nt((vdt_f * leave).astype(BF), later_low)
        both = jnp.sum((here * later).reshape(STATE // 8, 8, WIDE), axis=0)
        both = jnp.sum(both, axis=0, keepdims=True) * gains[c]
        both_high = both.astype(BF)
        both_low = (both - both_high.astype(F32)).astype(BF)
        through = mm(jnp.broadcast_to(both_high, (16, WIDE)), seg)
        through = through + mm(jnp.broadcast_to(both_low, (16, WIDE)), seg)
        dmix = dmix_ref[c]
        inner = [None] * (GROUP // 2)
        pairs = [vdt[:, 128 * j : 128 * (j + 1)] for j in range(GROUP // 2)]
        dparts = []
        for h in range(GROUP):
            dpair = dy[:, 128 * (h // 2) : 128 * (h // 2 + 1)]
            dparts.append(jnp.where(low if h % 2 == 0 else ~low, dpair, jnp.zeros_like(dpair)))
        following = mm_nt(pairs[0], dparts[0])
        for h in range(GROUP):
            dweights = following
            if h + 1 < GROUP:
                following = mm_nt(pairs[(h + 1) // 2], dparts[h + 1])
            gap = cumt_ref[0, h : h + 1, at] - cum[:, h : h + 1]
            decay = jnp.exp(jnp.minimum(gap, 0.0))
            weights = mixt_ref[c] * decay
            new = mm(weights.astype(BF), dparts[h])
            inner[h // 2] = new if inner[h // 2] is None else inner[h // 2] + new
            dmix = dmix + dweights * decay
            moved = (dweights * weights).astype(BF)
            turn = turn + mm(moved, select[h])
            across_ref[pl.ds(GROUP * local + h, 1), at] = jnp.sum(
                moved.astype(F32), axis=0, keepdims=True
            )
            if h == 1 and c + 1 < chunks:
                conv.chunk(c + 1)
        dmix_ref[c] = dmix
        dvdt = dvdt + jnp.concatenate(inner, axis=1)
        dcum_ref[at, :] += turn
        dpre = jnp.sum(sum_out, axis=0, keepdims=True) + through[0:1, :]
        dpre_ref[8 * c : 8 * c + 1, :] += dpre
        dstep_ref[at, :] += mm((act * dvdt).astype(BF), seg)
        conv.put(c, step_wide * dvdt + skip * dy_f)
        later = gains[c] * later + radd_ref[c].astype(F32)

    conv.chunk(0)
    conv.finish(dtaps_ref)

    @pl.when(local == pl.num_programs(0) - 1)
    def _():
        for c in range(chunks):
            at = pl.ds(c * SPAN, SPAN)
            dmix = jnp.where(tri(False), dmix_ref[c], 0.0).astype(BF)
            dkq_ref[at, :STATE] += mm(dmix, kq_ref[at, STATE:])
            dkq_ref[at, STATE:] += mm_tn(dmix, kq_ref[at, :STATE])


def last_kernel(*refs):
    parts = [refs[5 * k : 5 * k + 5] for k in range(len(CALLS))]
    (
        raw_ref, step_ref, hp_ref, proj_ref, slope_ref, taps_ref, masks_ref,
        dproj_ref, dtaps_ref, sums_ref, g_ref,
    ) = refs[5 * len(CALLS) :]
    rows = raw_ref.shape[0]
    upper = jnp.where(tri(False), 1.0, 0.0).astype(F32)
    rate = jnp.exp(hp_ref[1:2, :])
    d_log = jnp.zeros((1, 128), F32)
    d_bias = jnp.zeros((1, 128), F32)
    dproj_ref[pl.ds(0, HALO), pl.ds(WIDE, 128)] = jnp.zeros((HALO, 128), BF)

    def added_up(k, at, cols=slice(None)):
        total = parts[0][k][at, cols]
        for part in parts[1:]:
            total = total + part[k][at, cols]
        return total

    conv = ConvBack(
        proj_ref, slope_ref, g_ref, taps_ref, masks_ref, dproj_ref.at[:, pl.ds(0, WIDE)]
    )
    for c in reversed(range(rows // SPAN)):
        conv.put(c, added_up(0, pl.ds(c * SPAN, SPAN)))
        conv.chunk(c)
    conv.finish(dtaps_ref)
    for c in range(rows // SPAN):
        at = pl.ds(c * SPAN, SPAN)
        across = jnp.concatenate([part[2][:, at] for part in parts], axis=0)
        across = jnp.concatenate([across, jnp.zeros((128 - HEADS, SPAN), F32)], axis=0)
        turn = across.T + added_up(1, at)
        ddecay = jnp.dot(upper, turn, precision=EXACT, preferred_element_type=F32)
        ddecay = ddecay + added_up(3, pl.ds(8 * c, 1))
        step = step_ref[at, :]
        d_log = d_log - jnp.sum(ddecay * step * rate, axis=0, keepdims=True)
        draw = added_up(4, at) - ddecay * rate
        draw = draw * jax.nn.sigmoid(raw_ref[at, :] + hp_ref[0:1, :])
        draw = jnp.where(iota((SPAN, 128), 1) < HEADS, draw, 0.0)
        d_bias = d_bias + jnp.sum(draw, axis=0, keepdims=True)
        dproj_ref[pl.ds(HALO + c * SPAN, SPAN), pl.ds(WIDE, 128)] = draw.astype(BF)
    sums_ref[...] = jnp.zeros_like(sums_ref)
    sums_ref[0:1, :] = d_log
    sums_ref[1:2, :] = d_bias


def values_kernel(me_ref, part_ref, *refs):
    dprojs, wcs, out_ref = refs[: len(CALLS)], refs[len(CALLS) : len(CALLS) + 4], refs[-1]
    me = me_ref[0]
    size = part_ref.shape[0]
    quarter = wcs[0].shape[0]
    start = pl.multiple_of(HALO + pl.program_id(0) * size, HALO)
    for flip in range(4):
        own = pl.ds(pl.multiple_of((me ^ flip) * quarter, quarter), quarter)
        total = part_ref[:, own]
        first = 0
        for dproj_ref in dprojs:
            width = dproj_ref.shape[1]
            total = total + mm_nt(
                dproj_ref[pl.ds(start, size), :], wcs[flip][:, pl.ds(first, width)]
            )
            first += width
        out_ref[:, own] = total


def tokens_kernel(
    me_ref, tokens_ref, cot_ref, gain_ref, part_ref, dlast_ref, back_ref, w0, w1, w2, w3, d0, d1,
    d2, d3, grad_ref, dgain_ref, gn_ref,
):
    c = pl.program_id(0)
    me = me_ref[0]
    size, model = tokens_ref.shape
    quarter = model // 4
    start = pl.multiple_of(HALO + c * size, HALO)
    wcs, dts = (w0, w1, w2, w3), (d0, d1, d2, d3)

    @pl.when(c == 0)
    def _():
        dgain_ref[...] = jnp.zeros_like(dgain_ref)

    for flip in range(4):
        own = pl.ds(pl.multiple_of((me ^ flip) * quarter, quarter), quarter)
        total = part_ref[:, own] + mm_nt(
            dlast_ref[pl.ds(start, size), pl.ds(0, WIDE)], wcs[flip][:, pl.ds(INNER, WIDE)]
        )
        total = total + mm(
            dlast_ref[pl.ds(start, size), pl.ds(WIDE, 128)],
            dts[flip][pl.ds(0, 128), pl.ds(0, quarter)],
        )
        gn_ref[:, own] = total

    @pl.when(c == pl.num_programs(0) - 1)
    def _():
        for flip in range(4):
            own = pl.ds(pl.multiple_of((me ^ flip) * quarter, quarter), quarter)
            gn_ref[pl.ds(size - HALO, HALO), own] += mm_nt(back_ref[...], wcs[flip][...])

    hidden = tokens_ref[...].astype(F32)
    inv = lax.rsqrt(jnp.mean(hidden * hidden, axis=-1, keepdims=True) + EPSILON)
    gn = gn_ref[...]
    scaled = hidden * inv
    dgain_ref[0:1, :] += jnp.sum(gn * scaled, axis=0, keepdims=True)
    pulled = gn * gain_ref[...]
    mean = jnp.mean(pulled * scaled, axis=-1, keepdims=True)
    grad_ref[...] = cot_ref[...].astype(F32) + inv * (pulled - scaled * mean)


def whole(shape):
    zeros = (0,) * len(shape)
    return pl.BlockSpec(shape, lambda i: zeros)


def scalar():
    return pl.BlockSpec(memory_space=pltpu.SMEM)


def sds(shape, dtype):
    return jax.ShapeDtypeStruct(shape, dtype)


def passed_along(value, steps):
    count = lax.axis_size("shard")
    pairs = [(a, a + steps) for a in range(count) if 0 <= a + steps < count]
    return lax.ppermute(value, "shard", pairs)


def swap(value, axis, bit):
    count = lax.axis_size(axis)
    return lax.ppermute(value, axis, [(a, a ^ bit) for a in range(count)])


def gather_pieces(mine):
    across = swap(mine, "shard", 2)
    return mine, swap(mine, "shard", 1), across, swap(across, "shard", 1)


def gather_first(mine):
    return mine, swap(mine, "shard", 1), swap(mine, "shard", 2)


def rep_bits():
    size = lax.axis_size("rep")
    return [1 << b for b in range(size.bit_length() - 1)]


def row_steps(keep, give, scattered):
    keep = lax.optimization_barrier(keep)
    (give,) = yield (give,)
    rows = keep.shape[0] // 2
    chip = keep + swap(give, "shard", 1).astype(F32)
    held, sent = yield (chip[:rows], chip[rows:].astype(BF))
    held = held + swap(sent, "shard", 2).astype(F32)
    rep = lax.axis_index("rep")
    bits = rep_bits()
    for bit in bits[:scattered]:
        at = (rep & bit) // bit
        half = held.shape[0] // 2
        kept = lax.dynamic_slice_in_dim(held, at * half, half, 0)
        sent = lax.dynamic_slice_in_dim(held, (1 - at) * half, half, 0).astype(BF)
        kept, sent = yield (kept, sent)
        held = kept + swap(sent, "rep", bit).astype(F32)
    held = held.astype(BF)
    for bit in bits[scattered:]:
        (held,) = yield (held,)
        held = (held.astype(F32) + swap(held, "rep", bit).astype(F32)).astype(BF)
    for bit in reversed(bits[:scattered]):
        (held,) = yield (held,)
        at = (rep & bit) // bit
        other = swap(held, "rep", bit)
        held = jnp.concatenate(
            [jnp.where(at == 0, held, other), jnp.where(at == 0, other, held)], axis=0
        )
    yield (held,)


class RowSum:
    def __init__(self, keep, give, scattered):
        self.steps = row_steps(keep, give, scattered)
        self.waiting = next(self.steps)

    def take(self, values):
        try:
            self.waiting = self.steps.send(values)
        except StopIteration:
            self.waiting = values

    def result(self):
        for _ in range(16):
            self.take(self.waiting)
        return self.waiting[0].astype(F32)


def ordered(value, *sums):
    out = lax.optimization_barrier((value,) + tuple(one.waiting for one in sums))
    for one, values in zip(sums, out[1:]):
        one.take(values)
    return out[0]


def reduce_small(vector):
    for bit in (1, 2):
        vector = vector + swap(vector, "shard", bit)
    for bit in rep_bits():
        vector = vector + swap(vector, "rep", bit)
    return vector


def on_device(
    tokens, segments, norm_gain, in_weight, dt_weight, conv_weight, conv_bias, dt_bias, a_log,
    d_skip, gate_gain, out_weight, cotangent,
):
    rows, model = tokens.shape
    ext = rows + HALO
    chunks = rows // SPAN
    mine_conv = conv_bias.shape[0]
    conv = 4 * mine_conv
    me = lax.axis_index("shard")
    at_me = me.astype(jnp.int32).reshape(1)

    token_edge = passed_along(tokens[-HALO:], 1)
    prior = passed_along(segments[-8:] + 1, 1) - 1
    def line(*parts):
        flat = jnp.concatenate([part.reshape(-1) for part in parts])
        return jnp.pad(flat, (0, mine_conv - flat.shape[0]))[None]

    turned_dt = jnp.pad(dt_weight.T, ((0, 128 - HEADS), (0, mine_conv - dt_weight.shape[0])))
    packed = jnp.concatenate(
        [turned_dt, conv_weight.T, conv_bias[None], line(gate_gain), line(norm_gain),
         line(dt_bias, a_log, d_skip)], axis=0
    )
    packs = gather_pieces(packed)
    conv_columns, across, token_edge, prior = lax.optimization_barrier(
        (in_weight[:, INNER:], packs[2], token_edge, prior)
    )
    packs = packs[:2] + (across, packs[3])
    wc = gather_first(conv_columns)
    own, beside, far, corner = [part[128:] for part in packs]
    core, side = (me & 1) == 0, (me & 2) == 0
    left, right = jnp.where(core, own, beside), jnp.where(core, beside, own)
    up, down = jnp.where(core, far, corner), jnp.where(core, corner, far)
    pieces = [
        jnp.where(side, left, up), jnp.where(side, right, down),
        jnp.where(side, up, left), jnp.where(side, down, right),
    ]
    tables = jnp.stack(pieces).astype(F32)
    taps = jnp.concatenate(pieces, axis=1).astype(F32)
    gate_row = tables[:, 5, : gate_gain.shape[0]].reshape(1, INNER)
    norm_row = tables[:, 6, : norm_gain.shape[0]].reshape(1, model)
    per_head = HEADS // 4
    hp = tables[:, 7, : 3 * per_head].reshape(4, 3, per_head).transpose(1, 0, 2).reshape(3, HEADS)
    hp = jnp.pad(hp, ((0, 5), (0, 128 - HEADS)))
    spare = 128 - (24 + rows) % 128
    blank = jnp.full((16,), -1, jnp.int32)
    docs = jnp.concatenate([blank, prior, segments, jnp.full((spare,), -1, jnp.int32)])
    docs = docs.astype(F32)[None]

    gate_columns = in_weight[:, :INNER]

    half = model // 2
    xk, xg, plain = pl.pallas_call(
        norm_kernel,
        grid=(1,),
        in_specs=[scalar(), whole((HALO, model)), whole((rows, model)), whole((1, model))],
        out_specs=[whole((ext, half)), whole((ext, half)), whole((rows, model))],
        out_shape=[sds((ext, half), BF), sds((ext, half), BF), sds((rows, model), BF)],
        compiler_params=params(),
        cost_estimate=cost(4),
        name="norm_in",
    )(at_me, token_edge, tokens, norm_row)

    taps, hp, docs, gate_columns, xk, xg, plain, wc_far = lax.optimization_barrier(
        (taps, hp, docs, gate_columns, xk, xg, plain, wc[2])
    )
    wc = wc[:2] + (wc_far, swap(wc_far, "shard", 1))
    wg = gather_first(gate_columns)
    wide_rows = out_weight.shape[0] // 2
    kq_block = INNER // WIDE
    quarter = model // 4
    whole_x = [whole((ext, half)), whole((ext, half))]
    head_table = whole((rows, 128))
    proj_kq, kq, slope_kq, turned, raw, step, cum, cumt, mix, mixt, masks, run, step2, enter2, leave2, give2 = pl.pallas_call(
        first_kernel,
        grid=(1,),
        in_specs=whole_x
        + [pl.BlockSpec((quarter, WIDE), lambda i: (0, kq_block))] * 4
        + [whole(packed.shape)] * 4
        + [
            pl.BlockSpec((8, WIDE), lambda i: (0, kq_block)), whole((8, 128)),
            whole(docs.shape),
        ],
        out_specs=[
            whole((ext, WIDE)), whole((rows, WIDE)), whole((rows, WIDE)), whole((WIDE, rows)),
            head_table, head_table, head_table, whole((GROUPS, GROUP, rows)),
            whole((chunks, SPAN, SPAN)), whole((chunks, SPAN, SPAN)), whole((ext, 8)),
            whole((8, 128)), head_table, head_table, head_table, head_table,
        ],
        out_shape=[
            sds((ext, WIDE), BF), sds((rows, WIDE), BF), sds((rows, WIDE), BF),
            sds((WIDE, rows), BF), sds((rows, 128), F32), sds((rows, 128), F32),
            sds((rows, 128), F32), sds((GROUPS, GROUP, rows), F32),
            sds((chunks, SPAN, SPAN), F32), sds((chunks, SPAN, SPAN), F32), sds((ext, 8), F32),
            sds((8, 128), F32), sds((rows, 128), BF), sds((rows, 128), BF), sds((rows, 128), BF),
            sds((rows, 128), BF),
        ],
        scratch_shapes=[pltpu.VMEM((ext, WIDE), F32), pltpu.VMEM((docs.shape[1], 1), F32)],
        compiler_params=params(),
        cost_estimate=cost(8),
        name="keys_queries",
    )(xk, xg, *wc, *packs, taps, hp, docs)

    def columns(height, base=0):
        return pl.BlockSpec((height, WIDE), lambda i: (0, i + base))

    def states(base=0):
        return pl.BlockSpec((chunks, STATE, WIDE), lambda i: (0, 0, i + base))

    def cumt_spec(base=0):
        return pl.BlockSpec((1, GROUP, rows), lambda i: (i + base, 0, 0))

    run, wo_top = lax.optimization_barrier((run, out_weight[:wide_rows]))
    wo_a = gather_first(wo_top)
    proj_v, act, slope_v, adds, last = pl.pallas_call(
        state_kernel,
        grid=(GROUPS,),
        in_specs=whole_x + [columns(quarter)] * 4 + [
            columns(8), whole((ext, 8)), head_table, head_table, whole((WIDE, rows)),
        ],
        out_specs=[columns(ext), columns(rows), columns(rows), states(), columns(STATE)],
        out_shape=[
            sds((ext, INNER), BF), sds((rows, INNER), BF), sds((rows, INNER), BF),
            sds((chunks, STATE, INNER), BF), sds((STATE, INNER), BF),
        ],
        scratch_shapes=[pltpu.VMEM((ext, WIDE), F32)],
        compiler_params=params(),
        cost_estimate=cost(20),
        name="values_states",
    )(xk, xg, *wc, taps, masks, give2, cum, turned)

    wg_far, wo_far, last, act, adds, proj_v, slope_v = lax.optimization_barrier(
        (wg[2], wo_a[2], last, act, adds, proj_v, slope_v)
    )
    wg = wg[:2] + (wg_far, swap(wg_far, "shard", 1))
    wo_a = wo_a[:2] + (wo_far, swap(wo_far, "shard", 1))
    run_prev, run_next = passed_along(run, 1), passed_along(run, -1)
    near, far = passed_along(last, 1), passed_along(last, 2)

    inside, gate = pl.pallas_call(
        inside_kernel,
        grid=(GROUPS,),
        in_specs=whole_x + [columns(quarter)] * 4 + [
            columns(rows), head_table, head_table, cumt_spec(), whole((chunks, SPAN, SPAN)),
            whole((8, 128)),
        ],
        out_specs=[columns(rows), columns(rows)],
        out_shape=[sds((rows, INNER), F32), sds((rows, INNER), BF)],
        compiler_params=params(),
        cost_estimate=cost(20),
        name="scan_inside",
    )(xk, xg, *wg, act, step2, cum, cumt, mix, hp)

    near, far, run_prev, inside, gate, wo_low = lax.optimization_barrier(
        (near, far, run_prev, inside, gate, out_weight[wide_rows:])
    )
    wo_b = gather_first(wo_low)
    y, mixed, rms, into = pl.pallas_call(
        mixed_kernel,
        grid=(GROUPS,),
        in_specs=[
            columns(rows), columns(rows), whole((rows, WIDE)), head_table, head_table, states(),
            columns(STATE), columns(STATE), whole((8, 128)), whole((1, INNER)),
        ],
        out_specs=[columns(rows), whole((rows, INNER)), head_table, columns(STATE)],
        out_shape=[
            sds((rows, INNER), BF), sds((rows, INNER), BF), sds((rows, 128), F32),
            sds((STATE, INNER), F32),
        ],
        scratch_shapes=[
            pltpu.VMEM((GROUPS, rows, WIDE), F32), pltpu.VMEM((rows, 128), F32),
        ],
        compiler_params=params(),
        cost_estimate=cost(10),
        name="scan_gate",
    )(inside, gate, kq, enter2, cum, adds, near, far, run_prev, gate_row)
    wo_far, y, mixed, rms, into = lax.optimization_barrier((wo_b[2], y, mixed, rms, into))
    wo_b = wo_b[:2] + (wo_far, swap(wo_far, "shard", 1))
    wo = [part for both in zip(wo_a, wo_b) for part in both]

    def by_chunk(width):
        return pl.BlockSpec((SPAN, width), lambda c: (c, 0))

    grad_out = mm_tn(mixed, cotangent).astype(BF)
    grad_out, cum_then = lax.optimization_barrier((grad_out, cum))
    sum_out = lax.psum_scatter(grad_out, "shard", scatter_dimension=0, tiled=True)
    wo_specs = [whole((wide_rows, model))] * 8

    dy, dgate, dgain, dskip, radds, first = pl.pallas_call(
        gate_back_kernel,
        grid=(chunks,),
        in_specs=[scalar(), by_chunk(model)] + wo_specs + [
            by_chunk(INNER), by_chunk(INNER), by_chunk(128), whole((1, INNER)), by_chunk(INNER),
            pl.BlockSpec((WIDE, SPAN), lambda c: (0, c)), by_chunk(128), by_chunk(128),
        ],
        out_specs=[
            by_chunk(INNER), by_chunk(INNER), whole((8, INNER)), whole((8, INNER)),
            pl.BlockSpec((1, STATE, INNER), lambda c: (c, 0, 0)), whole((STATE, INNER)),
        ],
        out_shape=[
            sds((rows, INNER), BF), sds((rows, INNER), BF), sds((8, INNER), F32),
            sds((8, INNER), F32), sds((chunks, STATE, INNER), BF), sds((STATE, INNER), BF),
        ],
        scratch_shapes=[
            pltpu.VMEM((SPAN, INNER), F32), pltpu.VMEM((8, 128), F32),
            pltpu.VMEM((STATE, INNER), F32),
        ],
        compiler_params=params(),
        cost_estimate=cost(22),
        name="gate_back",
    )(at_me, cotangent, *wo, y, gate, rms, gate_row, act, turned, enter2, cum_then)

    grad_gate = mm_tn(plain, dgate).astype(BF)
    near, far = passed_along(first, -1), passed_along(first, -2)
    grad_gate, mixed_then = lax.optimization_barrier((grad_gate, mixed))
    sum_gate = lax.psum_scatter(grad_gate, "shard", scatter_dimension=0, tiled=True)
    output, part = pl.pallas_call(
        rows_kernel,
        grid=(chunks,),
        in_specs=[scalar(), by_chunk(INNER), by_chunk(model), by_chunk(INNER)] + wo_specs
        + [whole((quarter, INNER))] * 4,
        out_specs=[by_chunk(model), by_chunk(model)],
        out_shape=[sds((rows, model), BF), sds((rows, model), F32)],
        compiler_params=params(),
        cost_estimate=cost(18),
        name="rows_out",
    )(at_me, mixed_then, tokens, dgate, *wo, *wg)
    near, far, output, part, run_next, sum_out = lax.optimization_barrier(
        (near, far, output, part, run_next, sum_out)
    )
    sum_out = lax.psum(sum_out, "rep")

    dprojs, dtaps, partials = [], [], []
    sums = []

    def add_sum(parts, scattered):
        grad = parts[0] if len(parts) == 1 else jnp.concatenate(parts, axis=1)
        sums.append(RowSum(mm_tn(xk, grad), mm_tn(xg, grad).astype(BF), scattered))

    cum_then, output = lax.optimization_barrier((cum, output))
    for k, count in enumerate(CALLS):
        base = sum(CALLS[:k])
        width = count * WIDE
        dproj, dtap, *rest = pl.pallas_call(
            partial(scan_back_kernel, base),
            grid=(count,),
            in_specs=[
                whole((rows, WIDE)), whole((chunks, SPAN, SPAN)), head_table, head_table,
                head_table, head_table, cumt_spec(base), columns(rows, base), columns(rows, base),
                states(base), states(base), columns(STATE, base), columns(STATE, base),
                columns(STATE, base), whole((8, 128)), whole((8, 128)), columns(ext, base),
                columns(rows, base), columns(8, base), whole((ext, 8)),
            ],
            out_specs=[
                columns(ext), columns(8), whole((rows, WIDE)), head_table,
                whole((GROUP * count, rows)), whole((8 * chunks, 128)), head_table,
            ],
            out_shape=[
                sds((ext, width), BF), sds((8, width), F32), sds((rows, WIDE), F32),
                sds((rows, 128), F32), sds((GROUP * count, rows), F32),
                sds((8 * chunks, 128), F32), sds((rows, 128), F32),
            ],
            scratch_shapes=[
                pltpu.VMEM((ext + 8, WIDE), F32), pltpu.VMEM((chunks, SPAN, SPAN), F32),
                pltpu.VMEM((chunks, STATE, WIDE), F32),
            ],
            compiler_params=params(),
            cost_estimate=cost(15),
            name="scan_back",
        )(kq, mixt, step2, enter2, leave2, cum_then, cumt, act, dy, adds, radds, into, near, far,
          run_next, hp, proj_v, slope_v, taps, masks)
        if k == 0:
            sum_gate, dproj = lax.optimization_barrier((sum_gate, dproj))
            sum_gate = lax.psum(sum_gate, "rep")
        dproj, dtap, rest = ordered((dproj, dtap, rest), *sums)
        dprojs.append(dproj)
        dtaps.append(dtap)
        partials.extend(rest)
        add_sum([dproj], 2 if k == 0 else 1)
        cum_then, raw_then = ordered((cum, raw), sums[-1])

    tail = WIDE + 128
    dlast, dtap, head_sums = pl.pallas_call(
        last_kernel,
        grid=(1,),
        in_specs=[
            spec
            for count in CALLS
            for spec in (
                whole((rows, WIDE)), head_table, whole((GROUP * count, rows)),
                whole((8 * chunks, 128)), head_table,
            )
        ] + [
            head_table, head_table, whole((8, 128)), whole((ext, WIDE)), whole((rows, WIDE)),
            pl.BlockSpec((8, WIDE), lambda i: (0, kq_block)), whole((ext, 8)),
        ],
        out_specs=[whole((ext, tail)), whole((8, WIDE)), whole((8, 128))],
        out_shape=[sds((ext, tail), BF), sds((8, WIDE), F32), sds((8, 128), F32)],
        scratch_shapes=[pltpu.VMEM((ext + 8, WIDE), F32)],
        compiler_params=params(),
        cost_estimate=cost(8),
        name="last_back",
    )(*partials, raw_then, step, hp, proj_kq, slope_kq, taps, masks)
    dlast, dtap, head_sums = ordered((dlast, dtap, head_sums), *sums)
    dprojs.append(dlast)
    dtaps.append(dtap)

    add_sum(dprojs[3:], 0)
    part = ordered(part, sums[3])
    heads = jnp.concatenate([p[:HALO] for p in dprojs[:3]] + [dlast[:HALO, :WIDE]], axis=1)
    back = passed_along(heads, -1)
    value_part = pl.pallas_call(
        values_kernel,
        grid=(chunks,),
        in_specs=[scalar(), by_chunk(model)]
        + [whole((ext, count * WIDE)) for count in CALLS]
        + [pl.BlockSpec((quarter, INNER), lambda c: (0, 0))] * 4,
        out_specs=by_chunk(model),
        out_shape=sds((rows, model), F32),
        compiler_params=params(),
        cost_estimate=cost(10),
        name="values_back",
    )(at_me, part, *dprojs[:3], *wc)
    value_part, back = ordered((value_part, back), *sums)
    grad_tokens, g_norm = pl.pallas_call(
        tokens_kernel,
        grid=(chunks,),
        in_specs=[scalar(), by_chunk(model), by_chunk(model), whole((1, model)), by_chunk(model)]
        + [whole((ext, tail)), whole((HALO, conv))]
        + [whole((quarter, conv))] * 4
        + [whole(packed.shape)] * 4,
        out_specs=[by_chunk(model), whole((8, model))],
        out_shape=[sds((rows, model), F32), sds((8, model), F32)],
        scratch_shapes=[pltpu.VMEM((SPAN, model), F32)],
        compiler_params=params(),
        cost_estimate=cost(8),
        name="tokens_back",
    )(at_me, tokens, cotangent, norm_row, value_part, dlast, back, *wc, *packs)

    grad_tokens, g_norm = ordered((grad_tokens, g_norm), *sums)
    sum_out, sum_gate = ordered((sum_out, sum_gate), *sums)
    dtaps = jnp.concatenate(dtaps, axis=1)
    g_skip = jnp.sum(dskip[0].reshape(HEADS, HEAD_DIM), axis=1)
    parts = (
        g_norm[0], dtaps[:KW].T.reshape(-1), dtaps[KW], head_sums[1, :HEADS],
        head_sums[0, :HEADS], g_skip, dgain[0],
    )
    total = reduce_small(jnp.concatenate(parts))
    sums = [one.result() for one in sums]
    outs, start = [], 0
    for part in parts:
        size = part.shape[0] // 4
        outs.append(lax.dynamic_slice(total, (start + me * size,), (size,)))
        start += part.shape[0]
    s_norm, s_conv, s_cbias, s_step, s_decay, s_skip, s_gate = outs
    s_in = jnp.concatenate([sum_gate.astype(F32)] + sums[:3] + [sums[3][:, :WIDE]], axis=1)
    s_dt = sums[3][:, WIDE : WIDE + HEADS]
    return (
        output, grad_tokens, s_norm, s_in, s_dt, s_conv.reshape(-1, KW), s_cbias, s_step, s_decay,
        s_skip, s_gate, sum_out.astype(F32),
    )


def solution(mesh):
    spread = P(("rep", "shard"), None)
    row = P("shard")
    table = P("shard", None)
    return jax.shard_map(
        on_device,
        mesh=mesh,
        in_specs=(
            spread, P(("rep", "shard")), row, table, table, table, row, row, row, row, row, table,
            spread,
        ),
        out_specs=(
            spread, spread, row, table, table, table, row, row, row, row, row, table,
        ),
        check_vma=False,
    )
```

```python
from functools import partial

import jax
import jax.numpy as jnp
from jax import lax
from jax.experimental import pallas as pl
from jax.experimental.pallas import tpu as pltpu
from jax.sharding import PartitionSpec as P

HEADS = 32
HEAD_DIM = 64
STATE = 128
KW = 4
SPAN = 256
INNER = 2048
GROUP = 4
WIDE = GROUP * HEAD_DIM
GROUPS = HEADS // GROUP
ORDER = (0, 2, 1, 3)
CALLS = (4, 2, 2)
HALO = 16
CUT = -200.0
EPSILON = 1e-05
EXACT = lax.Precision.HIGHEST
BF = jnp.bfloat16
F32 = jnp.float32
VMEM = 56 * 1024 * 1024


def params():
    return pltpu.CompilerParams(vmem_limit_bytes=VMEM)


def cost(micros):
    return pl.CostEstimate(flops=int(micros * 2.0e7), bytes_accessed=0, transcendentals=0)


def mm(a, b):
    return jnp.dot(a, b, preferred_element_type=F32)


def mm_nt(a, b):
    return lax.dot_general(a, b, (((1,), (1,)), ((), ())), preferred_element_type=F32)


def mm_tn(a, b):
    return lax.dot_general(a, b, (((0,), (0,)), ((), ())), preferred_element_type=F32)


def iota(shape, dim):
    return lax.broadcasted_iota(jnp.int32, shape, dim)


def own_lanes(full, step):
    return pltpu.roll(full, lax.rem(128 - GROUP * step, 128), 1)


def pick_heads(step):
    row, col = iota((128, WIDE), 0), iota((128, WIDE), 1)
    wanted = GROUP * step + col // HEAD_DIM
    return jnp.where((row == wanted) | (row == wanted + HEADS), 1.0, 0.0).astype(BF)


def sum_heads(step):
    row, col = iota((WIDE, 128), 0), iota((WIDE, 128), 1)
    return jnp.where(GROUP * step + row // HEAD_DIM == col, 1.0, 0.0).astype(BF)


def two_parts(value):
    value = jnp.where(iota(value.shape, 1) < HEADS, value, 0.0)
    high = value.astype(BF).astype(F32)
    return (high + pltpu.roll(value - high, HEADS, 1)).astype(BF)


def tri(lower):
    a, b = iota((SPAN, SPAN), 0), iota((SPAN, SPAN), 1)
    return (a >= b) if lower else (a <= b)


def norm_kernel(me_ref, edge_ref, tokens_ref, gain_ref, keep_ref, give_ref, plain_ref):
    rows, model = tokens_ref.shape
    quarter = model // 4
    me = me_ref[0]

    def one(ref, start, size, out):
        hidden = ref[pl.ds(start, size), :].astype(F32)
        inv = lax.rsqrt(jnp.mean(hidden * hidden, axis=-1, keepdims=True) + EPSILON)
        for place, flip in enumerate(ORDER):
            at = pl.ds(pl.multiple_of((me ^ flip) * quarter, quarter), quarter)
            part = ref[pl.ds(start, size), at].astype(F32) * inv * gain_ref[:, at]
            target = keep_ref if place < 2 else give_ref
            cols = pl.ds((place % 2) * quarter, quarter)
            target[pl.ds(out, size), cols] = part.astype(BF)
            if out >= HALO:
                plain_ref[pl.ds(start, size), at] = part.astype(BF)

    one(edge_ref, 0, HALO, 0)
    for c in range(rows // SPAN):
        one(tokens_ref, c * SPAN, SPAN, HALO + c * SPAN)


def project(xk_ref, xg_ref, w_refs, start, size):
    quarter = xk_ref.shape[1] // 2
    at = pl.ds(start, size)
    total = None
    for place, flip in enumerate(ORDER):
        x_ref = xk_ref if place < 2 else xg_ref
        part = mm(x_ref[at, pl.ds((place % 2) * quarter, quarter)], w_refs[flip][...])
        total = part if total is None else total + part
    return total


def conv_rows(p_ref, taps_ref, masks, c):
    total = jnp.broadcast_to(taps_ref[KW : KW + 1, :], (SPAN, p_ref.shape[1]))
    base = HALO - KW + 1 + c * SPAN
    for k in range(KW):
        part = taps_ref[k : k + 1, :] * p_ref[pl.ds(base + k, SPAN), :]
        if k < KW - 1:
            part = part * masks[:, k : k + 1]
        total = total + part
    return total


def project_conv(xk_ref, xg_ref, w_refs, taps_ref, masks_ref, proj_ref, act_ref, slope_ref, p_ref, c):
    at = pl.ds(c * SPAN, SPAN)
    up = pl.ds(HALO + c * SPAN, SPAN)
    if c == 0:
        edge = project(xk_ref, xg_ref, w_refs, 0, HALO).astype(BF)
        proj_ref[pl.ds(0, HALO), :] = edge
        p_ref[pl.ds(0, HALO), :] = edge.astype(F32)
    for d in (0, 1) if c == 0 else (c + 1,):
        if d * SPAN < act_ref.shape[0]:
            ahead = pl.ds(HALO + d * SPAN, SPAN)
            own = project(xk_ref, xg_ref, w_refs, HALO + d * SPAN, SPAN).astype(BF)
            proj_ref[ahead, :] = own
            p_ref[ahead, :] = own.astype(F32)
    cs = conv_rows(p_ref, taps_ref, masks_ref[up, :], c)
    sig = jax.nn.sigmoid(cs)
    act = cs * sig
    act_ref[at, :] = act.astype(BF)
    slope_ref[at, :] = (sig * (1.0 + cs - act)).astype(BF)
    return act


def first_kernel(
    xk_ref, xg_ref, w0, w1, w2, w3, d0, d1, d2, d3, taps_ref, hp_ref, line_ref,
    proj_ref, act_ref, slope_ref, turned_ref, raw_ref, step_ref, cum_ref, cumt_ref, mix_ref,
    mixt_ref, masks_ref, run_ref, step2_ref, enter2_ref, leave2_ref, give2_ref, p_ref, docs_ref,
):
    rows = act_ref.shape[0]
    ext = rows + HALO
    lower = tri(True)
    ones_lower = jnp.where(lower, 1.0, 0.0).astype(F32)
    for b in range(line_ref.shape[1] // 128):
        block = jnp.broadcast_to(line_ref[0:1, pl.ds(128 * b, 128)], (128, 128))
        docs_ref[pl.ds(128 * b, 128), :] = block.T[:, 0:1]
    here = docs_ref[pl.ds(8, ext), :]
    lane = iota((ext, 8), 1)
    inside = iota((ext, 1), 0) - HALO
    masks = jnp.zeros((ext, 8), F32)
    for k in range(KW - 1):
        back = docs_ref[pl.ds(8 - KW + 1 + k, ext), :] == here
        masks = masks + jnp.where((lane == k) & back, 1.0, 0.0)
        ahead = (docs_ref[pl.ds(8 + KW - 1 - k, ext), :] == here) & (inside + KW - 1 - k >= 0)
        masks = masks + jnp.where((lane == 4 + k) & ahead, 1.0, 0.0)
    masks_ref[...] = masks
    total = jnp.zeros((1, 128), F32)
    for c in range(rows // SPAN):
        at = pl.ds(c * SPAN, SPAN)
        up = pl.ds(HALO + c * SPAN, SPAN)
        act = project_conv(
            xk_ref, xg_ref, (w0, w1, w2, w3), taps_ref, masks_ref, proj_ref, act_ref, slope_ref,
            p_ref, c,
        )
        turned_ref[:, at] = act.T.astype(BF)
        act = act.astype(BF)
        keys, queries = act[:, :STATE], act[:, STATE:]
        mix_ref[c] = jnp.where(lower, mm_nt(queries, keys), 0.0)
        mixt_ref[c] = jnp.where(tri(False), mm_nt(keys, queries), 0.0)
        quarter = xk_ref.shape[1] // 2
        raw = jnp.zeros((SPAN, 128), F32)
        for place, flip in enumerate(ORDER):
            x_ref = xk_ref if place < 2 else xg_ref
            part = x_ref[up, pl.ds((place % 2) * quarter, quarter)]
            raw = raw + mm_nt(part, (d0, d1, d2, d3)[flip][pl.ds(0, 128), pl.ds(0, quarter)])
        raw_ref[at, :] = raw
        step = jax.nn.softplus(raw + hp_ref[0:1, :])
        step_ref[at, :] = step
        cut = 1.0 - masks_ref[up, KW - 2 : KW - 1]
        decays = -step * jnp.exp(hp_ref[1:2, :]) + CUT * cut
        cum = jnp.dot(ones_lower, decays, precision=EXACT, preferred_element_type=F32)
        cum_ref[at, :] = cum
        cumt = lax.dot_general(
            decays, ones_lower, (((0,), (1,)), ((), ())), precision=EXACT,
            preferred_element_type=F32,
        )
        for g in range(GROUPS):
            cumt_ref[g, :, at] = cumt[GROUP * g : GROUP * (g + 1), :]
        end = cum[SPAN - 1 : SPAN, :]
        total = total + end
        step2_ref[at, :] = two_parts(step)
        enter2_ref[at, :] = two_parts(jnp.exp(cum))
        leave = jnp.exp(end - cum)
        leave2_ref[at, :] = two_parts(leave)
        give2_ref[at, :] = two_parts(leave * step)
    run_ref[...] = jnp.broadcast_to(total, (8, 128))


def gain_row(cum_row, step):
    return mm(two_parts(jnp.exp(jnp.broadcast_to(cum_row, (16, 128)))), pick_heads(step))[0:1, :]


def state_kernel(
    xk_ref, xg_ref, w0, w1, w2, w3, taps_ref, masks_ref, give2_ref, cum_ref, turned_ref,
    proj_ref, act_ref, slope_ref, add_ref, last_ref, p_ref,
):
    rows = act_ref.shape[0]
    i = pl.program_id(0)
    pick = pick_heads(i)
    state = jnp.zeros((STATE, WIDE), F32)
    for c in range(rows // SPAN):
        at = pl.ds(c * SPAN, SPAN)
        act = project_conv(
            xk_ref, xg_ref, (w0, w1, w2, w3), taps_ref, masks_ref, proj_ref, act_ref, slope_ref,
            p_ref, c,
        )
        scale = mm(give2_ref[at, :], pick)
        new = mm(turned_ref[pl.ds(0, STATE), at], (act * scale).astype(BF))
        add_ref[c] = new.astype(BF)
        end = cum_ref[pl.ds(c * SPAN + SPAN - 1, 1), :]
        state = gain_row(end, i) * state + new
    last_ref[...] = state.astype(BF)


def inside_kernel(
    xk_ref, xg_ref, w0, w1, w2, w3, act_ref, step2_ref, cum_ref, cumt_ref, mix_ref, hp_ref,
    y_ref, gate_ref,
):
    rows = act_ref.shape[0]
    i = pl.program_id(0)
    low = iota((SPAN, 128), 1) < HEAD_DIM
    pick = pick_heads(i)
    skip = mm(two_parts(jnp.broadcast_to(hp_ref[2:3, :], (16, 128))), pick)[0:1, :]
    for c in range(rows // SPAN):
        at = pl.ds(c * SPAN, SPAN)
        gate_ref[at, :] = project(
            xk_ref, xg_ref, (w0, w1, w2, w3), HALO + c * SPAN, SPAN
        ).astype(BF)
        cum = own_lanes(cum_ref[at, :], i)
        act = act_ref[at, :].astype(F32)
        vdt = (act * mm(step2_ref[at, :], pick)).astype(BF)
        for j in range(GROUP // 2):
            cols = slice(128 * j, 128 * (j + 1))
            pair = vdt[:, cols]
            total = skip[:, cols] * act[:, cols]
            for s in range(2):
                h = 2 * j + s
                gap = cum[:, h : h + 1] - cumt_ref[0, h : h + 1, at]
                weights = (mix_ref[c] * jnp.exp(jnp.minimum(gap, 0.0))).astype(BF)
                part = jnp.where(low if s == 0 else ~low, pair, jnp.zeros_like(pair))
                total = total + mm(weights, part)
            y_ref[at, pl.ds(128 * j, 128)] = total.astype(BF)


def mixed_kernel(
    inside_ref, gate_ref, kq_ref, enter2_ref, cum_ref, add_ref, near_ref, far_ref, run_ref,
    gain_ref,
    y_ref, mixed_ref, rms_ref, into_ref, gated_ref, sum_ref,
):
    rows = inside_ref.shape[0]
    i = pl.program_id(0)
    pick = pick_heads(i)
    state = near_ref[...].astype(F32) + gain_row(run_ref[0:1, :], i) * far_ref[...].astype(F32)
    into_ref[...] = state

    @pl.when(i == 0)
    def _():
        sum_ref[...] = jnp.zeros_like(sum_ref)

    for c in range(rows // SPAN):
        at = pl.ds(c * SPAN, SPAN)
        y = mm(enter2_ref[at, :], pick) * mm(kq_ref[at, STATE:], state.astype(BF))
        y = y + inside_ref[at, :].astype(F32)
        y_ref[at, :] = y.astype(BF)
        wide = gate_ref[at, :].astype(F32)
        gated = y * (wide * jax.nn.sigmoid(wide))
        gated_ref[i, at, :] = gated
        squares = gated * gated
        sum_ref[at, :] += squares[:, :128] + squares[:, 128:]
        state = gain_row(cum_ref[pl.ds(c * SPAN + SPAN - 1, 1), :], i) * state + add_ref[c].astype(F32)

    @pl.when(i == GROUPS - 1)
    def _():
        for c in range(rows // SPAN):
            at = pl.ds(c * SPAN, SPAN)
            mean = jnp.sum(sum_ref[at, :], axis=1, keepdims=True) * (1.0 / INNER)
            rms = lax.rsqrt(mean + EPSILON)
            rms_ref[at, :] = jnp.broadcast_to(rms, (SPAN, 128))
            for g in range(GROUPS):
                cols = pl.ds(g * WIDE, WIDE)
                mixed_ref[at, cols] = (gated_ref[g, at, :] * rms * gain_ref[:, cols]).astype(BF)


def rows_kernel(me_ref, mixed_ref, tokens_ref, dgate_ref, *refs):
    wos, wgs = refs[:8], refs[8:12]
    out_ref, part_ref = refs[12:]
    me = me_ref[0]
    per = GROUPS // 4
    quarter = wgs[0].shape[0]
    total = tokens_ref[...].astype(F32)
    for flip in range(4):
        for s in range(per):
            cols = pl.ds(pl.multiple_of(((me ^ flip) * per + s) * WIDE, WIDE), WIDE)
            total = total + mm(mixed_ref[:, cols], wos[per * flip + s][...])
    out_ref[...] = total.astype(BF)
    for flip in range(4):
        own = pl.ds(pl.multiple_of((me ^ flip) * quarter, quarter), quarter)
        part_ref[:, own] = mm_nt(dgate_ref[...], wgs[flip][...])


def gate_back_kernel(
    me_ref, cot_ref, w0, w1, w2, w3, w4, w5, w6, w7, y_ref, gate_ref, mixed_ref, rms_ref, gain_ref,
    act_ref, turned_ref, enter2_ref, cum_ref,
    dy_ref, dgate_ref, dgain_ref, dskip_ref, add_ref, first_ref, gm_ref, run_ref, acc_ref,
):
    c = pl.program_id(0)
    me = me_ref[0]

    @pl.when(c == 0)
    def _():
        dgain_ref[...] = jnp.zeros_like(dgain_ref)
        dskip_ref[...] = jnp.zeros_like(dskip_ref)
        acc_ref[...] = jnp.zeros_like(acc_ref)
        run_ref[...] = jnp.zeros_like(run_ref)

    rms = rms_ref[:, 0:1]
    total = jnp.zeros((SPAN, 128), F32)
    cot = cot_ref[...]
    per = GROUPS // 4
    ws = (w0, w1, w2, w3, w4, w5, w6, w7)
    following = mm_nt(cot, ws[0][...])
    for flip in range(4):
        for s in range(per):
            cols = pl.ds(pl.multiple_of(((me ^ flip) * per + s) * WIDE, WIDE), WIDE)
            gm = following
            if per * flip + s + 1 < GROUPS:
                following = mm_nt(cot, ws[per * flip + s + 1][...])
            gm_ref[:, cols] = gm
            q = gm * mixed_ref[:, cols].astype(F32)
            total = total + q[:, :128] + q[:, 128:]
    mean = jnp.sum(total, axis=1, keepdims=True) * (1.0 / INNER)
    shrink = rms * rms * mean
    following = mm(enter2_ref[...], pick_heads(0))
    for g in range(GROUPS):
        cols = pl.ds(g * WIDE, WIDE)
        enter = following
        if g + 1 < GROUPS:
            following = mm(enter2_ref[...], pick_heads(g + 1))
        gm = gm_ref[:, cols]
        wide = gate_ref[:, cols].astype(F32)
        sig = jax.nn.sigmoid(wide)
        silu = wide * sig
        y = y_ref[:, cols].astype(F32)
        gated = y * silu
        dgain_ref[0:1, cols] += jnp.sum(gm * gated * rms, axis=0, keepdims=True)
        dgated = rms * (gm * gain_ref[:, cols]) - gated * shrink
        dy = dgated * silu
        dy_ref[:, cols] = dy.astype(BF)
        dgate_ref[:, cols] = (dgated * y * (sig * (1.0 + wide - silu))).astype(BF)
        dskip_ref[0:1, cols] += jnp.sum(dy * act_ref[:, cols].astype(F32), axis=0, keepdims=True)
        scaled = (dy * enter).astype(BF)
        new = mm(turned_ref[pl.ds(STATE, STATE), :], scaled)
        add_ref[0, :, cols] = new.astype(BF)
        acc_ref[:, cols] += gain_row(run_ref[0:1, :], g) * new
    run_ref[0:1, :] += cum_ref[SPAN - 1 : SPAN, :]

    @pl.when(c == pl.num_programs(0) - 1)
    def _():
        first_ref[...] = acc_ref[...].astype(BF)


class ConvBack:
    def __init__(self, proj_ref, slope_ref, g_ref, taps_ref, masks_ref, dproj_ref):
        self.refs = proj_ref, slope_ref, g_ref, taps_ref, masks_ref, dproj_ref
        self.rows, self.width = slope_ref.shape
        g_ref[pl.ds(0, HALO), :] = jnp.zeros((HALO, self.width), F32)
        g_ref[pl.ds(HALO + self.rows, 8), :] = jnp.zeros((8, self.width), F32)
        self.bias = jnp.zeros((8, self.width), F32)
        self.sums = [jnp.zeros((8, self.width), F32) for _ in range(KW)]

    def put(self, c, grad):
        _, slope_ref, g_ref, *_ = self.refs
        g = grad * slope_ref[pl.ds(c * SPAN, SPAN), :].astype(F32)
        g_ref[pl.ds(HALO + c * SPAN, SPAN), :] = g
        self.bias = self.bias + jnp.sum(g.reshape(SPAN // 8, 8, self.width), axis=0)

    def chunk(self, c):
        self.piece(HALO + c * SPAN, SPAN)

    def piece(self, start, size):
        proj_ref, _, g_ref, taps_ref, masks_ref, dproj_ref = self.refs
        at = pl.ds(start, size)
        x = proj_ref[at, :].astype(F32)
        total = None
        for k in range(KW):
            g = g_ref[pl.ds(start + KW - 1 - k, size), :]
            if k < KW - 1:
                g = g * masks_ref[at, 4 + k : 5 + k]
            part = taps_ref[k : k + 1, :] * g
            total = part if total is None else total + part
            self.sums[k] = self.sums[k] + jnp.sum((g * x).reshape(size // 8, 8, self.width), axis=0)
        dproj_ref[at, :] = total.astype(BF)

    def finish(self, dtaps_ref):
        self.piece(0, HALO)
        for k in range(KW):
            dtaps_ref[k : k + 1, :] = jnp.sum(self.sums[k], axis=0, keepdims=True)
        dtaps_ref[KW : KW + 1, :] = jnp.sum(self.bias, axis=0, keepdims=True)


def scan_back_kernel(
    base, kq_ref, mixt_ref, step2_ref, enter2_ref, leave2_ref, cum_ref, cumt_ref, act_ref, dy_ref,
    add_ref, radd_ref, into_ref, near_ref, far_ref, run_ref, hp_ref, proj_ref, slope_ref,
    taps_ref, masks_ref,
    dproj_ref, dtaps_ref, dkq_ref, dcum_ref, across_ref, dpre_ref, dstep_ref,
    g_ref, dmix_ref, s_ref,
):
    rows = act_ref.shape[0]
    chunks = rows // SPAN
    local = pl.program_id(0)
    i = local + base
    low = iota((SPAN, 128), 1) < HEAD_DIM
    pick = pick_heads(i)
    seg = sum_heads(i)
    skip = mm(two_parts(jnp.broadcast_to(hp_ref[2:3, :], (16, 128))), pick)[0:1, :]
    select = [
        jnp.where(iota((SPAN, 128), 1) == GROUP * i + h, -1.0, 0.0).astype(BF)
        for h in range(GROUP)
    ]

    @pl.when(local == 0)
    def _():
        dkq_ref[...] = jnp.zeros_like(dkq_ref)
        dcum_ref[...] = jnp.zeros_like(dcum_ref)
        dpre_ref[...] = jnp.zeros_like(dpre_ref)
        dstep_ref[...] = jnp.zeros_like(dstep_ref)
        dmix_ref[...] = jnp.zeros_like(dmix_ref)

    state = into_ref[...]
    gains = []
    for c in range(chunks):
        s_ref[c] = state
        gains.append(gain_row(cum_ref[pl.ds(c * SPAN + SPAN - 1, 1), :], i))
        state = gains[c] * state + add_ref[c].astype(F32)

    conv = ConvBack(proj_ref, slope_ref, g_ref, taps_ref, masks_ref, dproj_ref)
    later = near_ref[...].astype(F32) + gain_row(run_ref[0:1, :], i) * far_ref[...].astype(F32)
    for c in reversed(range(chunks)):
        at = pl.ds(c * SPAN, SPAN)
        cum = own_lanes(cum_ref[at, :], i)
        enter = mm(enter2_ref[at, :], pick)
        leave = mm(leave2_ref[at, :], pick)
        step_wide = mm(step2_ref[at, :], pick)
        act = act_ref[at, :].astype(F32)
        vdt_f = act * step_wide
        vdt = vdt_f.astype(BF)
        dy = dy_ref[at, :]
        dy_f = dy.astype(F32)
        keys, queries = kq_ref[at, :STATE], kq_ref[at, STATE:]
        here = s_ref[c]
        here_low, later_low = here.astype(BF), later.astype(BF)
        dys = dy_f * enter
        dvdt = leave * mm(keys, later_low)
        sum_out = mm((vdt_f * dvdt).astype(BF), seg)
        turn = mm((dys * mm(queries, here_low)).astype(BF), seg) - sum_out
        dkq_ref[at, STATE:] += mm_nt(dys.astype(BF), here_low)
        dkq_ref[at, :STATE] += mm_nt((vdt_f * leave).astype(BF), later_low)
        both = jnp.sum((here * later).reshape(STATE // 8, 8, WIDE), axis=0)
        both = jnp.sum(both, axis=0, keepdims=True) * gains[c]
        both_high = both.astype(BF)
        both_low = (both - both_high.astype(F32)).astype(BF)
        through = mm(jnp.broadcast_to(both_high, (16, WIDE)), seg)
        through = through + mm(jnp.broadcast_to(both_low, (16, WIDE)), seg)
        dmix = dmix_ref[c]
        inner = [None] * (GROUP // 2)
        pairs = [vdt[:, 128 * j : 128 * (j + 1)] for j in range(GROUP // 2)]
        dparts = []
        for h in range(GROUP):
            dpair = dy[:, 128 * (h // 2) : 128 * (h // 2 + 1)]
            dparts.append(jnp.where(low if h % 2 == 0 else ~low, dpair, jnp.zeros_like(dpair)))
        following = mm_nt(pairs[0], dparts[0])
        for h in range(GROUP):
            dweights = following
            if h + 1 < GROUP:
                following = mm_nt(pairs[(h + 1) // 2], dparts[h + 1])
            gap = cumt_ref[0, h : h + 1, at] - cum[:, h : h + 1]
            decay = jnp.exp(jnp.minimum(gap, 0.0))
            weights = mixt_ref[c] * decay
            new = mm(weights.astype(BF), dparts[h])
            inner[h // 2] = new if inner[h // 2] is None else inner[h // 2] + new
            dmix = dmix + dweights * decay
            moved = (dweights * weights).astype(BF)
            turn = turn + mm(moved, select[h])
            across_ref[pl.ds(GROUP * local + h, 1), at] = jnp.sum(
                moved.astype(F32), axis=0, keepdims=True
            )
            if h == 1 and c + 1 < chunks:
                conv.chunk(c + 1)
        dmix_ref[c] = dmix
        dvdt = dvdt + jnp.concatenate(inner, axis=1)
        dcum_ref[at, :] += turn
        dpre = jnp.sum(sum_out, axis=0, keepdims=True) + through[0:1, :]
        dpre_ref[8 * c : 8 * c + 1, :] += dpre
        dstep_ref[at, :] += mm((act * dvdt).astype(BF), seg)
        conv.put(c, step_wide * dvdt + skip * dy_f)
        later = gains[c] * later + radd_ref[c].astype(F32)

    conv.chunk(0)
    conv.finish(dtaps_ref)

    @pl.when(local == pl.num_programs(0) - 1)
    def _():
        for c in range(chunks):
            at = pl.ds(c * SPAN, SPAN)
            dmix = jnp.where(tri(False), dmix_ref[c], 0.0).astype(BF)
            dkq_ref[at, :STATE] += mm(dmix, kq_ref[at, STATE:])
            dkq_ref[at, STATE:] += mm_tn(dmix, kq_ref[at, :STATE])


def last_kernel(*refs):
    parts = [refs[5 * k : 5 * k + 5] for k in range(len(CALLS))]
    (
        raw_ref, step_ref, hp_ref, proj_ref, slope_ref, taps_ref, masks_ref,
        dproj_ref, dtaps_ref, sums_ref, g_ref,
    ) = refs[5 * len(CALLS) :]
    rows = raw_ref.shape[0]
    upper = jnp.where(tri(False), 1.0, 0.0).astype(F32)
    rate = jnp.exp(hp_ref[1:2, :])
    d_log = jnp.zeros((1, 128), F32)
    d_bias = jnp.zeros((1, 128), F32)
    dproj_ref[pl.ds(0, HALO), pl.ds(WIDE, 128)] = jnp.zeros((HALO, 128), BF)

    def added_up(k, at, cols=slice(None)):
        total = parts[0][k][at, cols]
        for part in parts[1:]:
            total = total + part[k][at, cols]
        return total

    conv = ConvBack(
        proj_ref, slope_ref, g_ref, taps_ref, masks_ref, dproj_ref.at[:, pl.ds(0, WIDE)]
    )
    for c in reversed(range(rows // SPAN)):
        conv.put(c, added_up(0, pl.ds(c * SPAN, SPAN)))
        conv.chunk(c)
    conv.finish(dtaps_ref)
    for c in range(rows // SPAN):
        at = pl.ds(c * SPAN, SPAN)
        across = jnp.concatenate([part[2][:, at] for part in parts], axis=0)
        across = jnp.concatenate([across, jnp.zeros((128 - HEADS, SPAN), F32)], axis=0)
        turn = across.T + added_up(1, at)
        ddecay = jnp.dot(upper, turn, precision=EXACT, preferred_element_type=F32)
        ddecay = ddecay + added_up(3, pl.ds(8 * c, 1))
        step = step_ref[at, :]
        d_log = d_log - jnp.sum(ddecay * step * rate, axis=0, keepdims=True)
        draw = added_up(4, at) - ddecay * rate
        draw = draw * jax.nn.sigmoid(raw_ref[at, :] + hp_ref[0:1, :])
        draw = jnp.where(iota((SPAN, 128), 1) < HEADS, draw, 0.0)
        d_bias = d_bias + jnp.sum(draw, axis=0, keepdims=True)
        dproj_ref[pl.ds(HALO + c * SPAN, SPAN), pl.ds(WIDE, 128)] = draw.astype(BF)
    sums_ref[...] = jnp.zeros_like(sums_ref)
    sums_ref[0:1, :] = d_log
    sums_ref[1:2, :] = d_bias


def values_kernel(me_ref, part_ref, *refs):
    dprojs, wcs, out_ref = refs[: len(CALLS)], refs[len(CALLS) : len(CALLS) + 4], refs[-1]
    me = me_ref[0]
    size = part_ref.shape[0]
    quarter = wcs[0].shape[0]
    start = pl.multiple_of(HALO + pl.program_id(0) * size, HALO)
    for flip in range(4):
        own = pl.ds(pl.multiple_of((me ^ flip) * quarter, quarter), quarter)
        total = part_ref[:, own]
        first = 0
        for dproj_ref in dprojs:
            width = dproj_ref.shape[1]
            total = total + mm_nt(
                dproj_ref[pl.ds(start, size), :], wcs[flip][:, pl.ds(first, width)]
            )
            first += width
        out_ref[:, own] = total


def tokens_kernel(
    me_ref, tokens_ref, cot_ref, gain_ref, part_ref, dlast_ref, back_ref, w0, w1, w2, w3, d0, d1,
    d2, d3, grad_ref, dgain_ref, gn_ref,
):
    c = pl.program_id(0)
    me = me_ref[0]
    size, model = tokens_ref.shape
    quarter = model // 4
    start = pl.multiple_of(HALO + c * size, HALO)
    wcs, dts = (w0, w1, w2, w3), (d0, d1, d2, d3)

    @pl.when(c == 0)
    def _():
        dgain_ref[...] = jnp.zeros_like(dgain_ref)

    for flip in range(4):
        own = pl.ds(pl.multiple_of((me ^ flip) * quarter, quarter), quarter)
        total = part_ref[:, own] + mm_nt(
            dlast_ref[pl.ds(start, size), pl.ds(0, WIDE)], wcs[flip][:, pl.ds(INNER, WIDE)]
        )
        total = total + mm(
            dlast_ref[pl.ds(start, size), pl.ds(WIDE, 128)],
            dts[flip][pl.ds(0, 128), pl.ds(0, quarter)],
        )
        gn_ref[:, own] = total

    @pl.when(c == pl.num_programs(0) - 1)
    def _():
        for flip in range(4):
            own = pl.ds(pl.multiple_of((me ^ flip) * quarter, quarter), quarter)
            gn_ref[pl.ds(size - HALO, HALO), own] += mm_nt(back_ref[...], wcs[flip][...])

    hidden = tokens_ref[...].astype(F32)
    inv = lax.rsqrt(jnp.mean(hidden * hidden, axis=-1, keepdims=True) + EPSILON)
    gn = gn_ref[...]
    scaled = hidden * inv
    dgain_ref[0:1, :] += jnp.sum(gn * scaled, axis=0, keepdims=True)
    pulled = gn * gain_ref[...]
    mean = jnp.mean(pulled * scaled, axis=-1, keepdims=True)
    grad_ref[...] = cot_ref[...].astype(F32) + inv * (pulled - scaled * mean)


def whole(shape):
    zeros = (0,) * len(shape)
    return pl.BlockSpec(shape, lambda i: zeros)


def scalar():
    return pl.BlockSpec(memory_space=pltpu.SMEM)


def sds(shape, dtype):
    return jax.ShapeDtypeStruct(shape, dtype)


def passed_along(value, steps):
    count = lax.axis_size("shard")
    pairs = [(a, a + steps) for a in range(count) if 0 <= a + steps < count]
    return lax.ppermute(value, "shard", pairs)


def swap(value, axis, bit):
    count = lax.axis_size(axis)
    return lax.ppermute(value, axis, [(a, a ^ bit) for a in range(count)])


def gather_pieces(mine):
    across = swap(mine, "shard", 2)
    return mine, swap(mine, "shard", 1), across, swap(across, "shard", 1)


def gather_first(mine):
    return mine, swap(mine, "shard", 1), swap(mine, "shard", 2)


def rep_bits():
    size = lax.axis_size("rep")
    return [1 << b for b in range(size.bit_length() - 1)]


def row_steps(keep, give, scattered):
    keep = lax.optimization_barrier(keep)
    (give,) = yield (give,)
    rows = keep.shape[0] // 2
    chip = keep + swap(give, "shard", 1).astype(F32)
    held, sent = yield (chip[:rows], chip[rows:].astype(BF))
    held = held + swap(sent, "shard", 2).astype(F32)
    rep = lax.axis_index("rep")
    bits = rep_bits()
    for bit in bits[:scattered]:
        at = (rep & bit) // bit
        half = held.shape[0] // 2
        kept = lax.dynamic_slice_in_dim(held, at * half, half, 0)
        sent = lax.dynamic_slice_in_dim(held, (1 - at) * half, half, 0).astype(BF)
        kept, sent = yield (kept, sent)
        held = kept + swap(sent, "rep", bit).astype(F32)
    held = held.astype(BF)
    for bit in bits[scattered:]:
        (held,) = yield (held,)
        held = (held.astype(F32) + swap(held, "rep", bit).astype(F32)).astype(BF)
    for bit in reversed(bits[:scattered]):
        (held,) = yield (held,)
        at = (rep & bit) // bit
        other = swap(held, "rep", bit)
        held = jnp.concatenate(
            [jnp.where(at == 0, held, other), jnp.where(at == 0, other, held)], axis=0
        )
    yield (held,)


class RowSum:
    def __init__(self, keep, give, scattered):
        self.steps = row_steps(keep, give, scattered)
        self.waiting = next(self.steps)

    def take(self, values):
        try:
            self.waiting = self.steps.send(values)
        except StopIteration:
            self.waiting = values

    def result(self):
        for _ in range(16):
            self.take(self.waiting)
        return self.waiting[0].astype(F32)


def ordered(value, *sums):
    out = lax.optimization_barrier((value,) + tuple(one.waiting for one in sums))
    for one, values in zip(sums, out[1:]):
        one.take(values)
    return out[0]


def reduce_small(vector, *read_then):
    for bit in (1, 2):
        vector = vector + swap(vector, "shard", bit)
    vector, *read_then = lax.optimization_barrier((vector,) + read_then)
    for bit in rep_bits():
        vector = vector + swap(vector, "rep", bit)
    return vector, *read_then


def on_device(
    tokens, segments, norm_gain, in_weight, dt_weight, conv_weight, conv_bias, dt_bias, a_log,
    d_skip, gate_gain, out_weight, cotangent,
):
    rows, model = tokens.shape
    ext = rows + HALO
    chunks = rows // SPAN
    mine_conv = conv_bias.shape[0]
    conv = 4 * mine_conv
    me = lax.axis_index("shard")
    at_me = me.astype(jnp.int32).reshape(1)

    def line(*parts):
        flat = jnp.concatenate([part.reshape(-1) for part in parts])
        return jnp.pad(flat, (0, mine_conv - flat.shape[0]))[None]

    turned_dt = jnp.pad(dt_weight.T, ((0, 128 - HEADS), (0, mine_conv - dt_weight.shape[0])))
    packed = jnp.concatenate(
        [turned_dt, conv_weight.T, conv_bias[None], line(gate_gain), line(norm_gain),
         line(dt_bias, a_log, d_skip)], axis=0
    )
    packed, token_edge, prior = lax.optimization_barrier(
        (packed, tokens[-HALO:], segments[-8:] + 1)
    )
    packs = gather_pieces(packed)
    token_edge = passed_along(token_edge, 1)
    prior = passed_along(prior, 1) - 1
    conv_columns, across, token_edge, prior = lax.optimization_barrier(
        (in_weight[:, INNER:], packs[2], token_edge, prior)
    )
    packs = packs[:2] + (across, packs[3])
    wc = gather_first(conv_columns)
    own, beside, far, corner = [part[128:] for part in packs]
    core, side = (me & 1) == 0, (me & 2) == 0
    left, right = jnp.where(core, own, beside), jnp.where(core, beside, own)
    up, down = jnp.where(core, far, corner), jnp.where(core, corner, far)
    pieces = [
        jnp.where(side, left, up), jnp.where(side, right, down),
        jnp.where(side, up, left), jnp.where(side, down, right),
    ]
    tables = jnp.stack(pieces).astype(F32)
    taps = jnp.concatenate(pieces, axis=1).astype(F32)
    gate_row = tables[:, 5, : gate_gain.shape[0]].reshape(1, INNER)
    norm_row = tables[:, 6, : norm_gain.shape[0]].reshape(1, model)
    per_head = HEADS // 4
    hp = tables[:, 7, : 3 * per_head].reshape(4, 3, per_head).transpose(1, 0, 2).reshape(3, HEADS)
    hp = jnp.pad(hp, ((0, 5), (0, 128 - HEADS)))
    spare = 128 - (24 + rows) % 128
    blank = jnp.full((16,), -1, jnp.int32)
    docs = jnp.concatenate([blank, prior, segments, jnp.full((spare,), -1, jnp.int32)])
    docs = docs.astype(F32)[None]

    gate_columns = in_weight[:, :INNER]

    half = model // 2
    xk, xg, plain = pl.pallas_call(
        norm_kernel,
        grid=(1,),
        in_specs=[scalar(), whole((HALO, model)), whole((rows, model)), whole((1, model))],
        out_specs=[whole((ext, half)), whole((ext, half)), whole((rows, model))],
        out_shape=[sds((ext, half), BF), sds((ext, half), BF), sds((rows, model), BF)],
        compiler_params=params(),
        cost_estimate=cost(4),
        name="norm_in",
    )(at_me, token_edge, tokens, norm_row)

    taps, hp, docs, gate_columns, xk, xg, plain, wc_far = lax.optimization_barrier(
        (taps, hp, docs, gate_columns, xk, xg, plain, wc[2])
    )
    wc = wc[:2] + (wc_far, swap(wc_far, "shard", 1))
    wg = gather_first(gate_columns)
    wide_rows = out_weight.shape[0] // 2
    kq_block = INNER // WIDE
    quarter = model // 4
    whole_x = [whole((ext, half)), whole((ext, half))]
    head_table = whole((rows, 128))
    proj_kq, kq, slope_kq, turned, raw, step, cum, cumt, mix, mixt, masks, run, step2, enter2, leave2, give2 = pl.pallas_call(
        first_kernel,
        grid=(1,),
        in_specs=whole_x
        + [pl.BlockSpec((quarter, WIDE), lambda i: (0, kq_block))] * 4
        + [whole(packed.shape)] * 4
        + [
            pl.BlockSpec((8, WIDE), lambda i: (0, kq_block)), whole((8, 128)),
            whole(docs.shape),
        ],
        out_specs=[
            whole((ext, WIDE)), whole((rows, WIDE)), whole((rows, WIDE)), whole((WIDE, rows)),
            head_table, head_table, head_table, whole((GROUPS, GROUP, rows)),
            whole((chunks, SPAN, SPAN)), whole((chunks, SPAN, SPAN)), whole((ext, 8)),
            whole((8, 128)), head_table, head_table, head_table, head_table,
        ],
        out_shape=[
            sds((ext, WIDE), BF), sds((rows, WIDE), BF), sds((rows, WIDE), BF),
            sds((WIDE, rows), BF), sds((rows, 128), F32), sds((rows, 128), F32),
            sds((rows, 128), F32), sds((GROUPS, GROUP, rows), F32),
            sds((chunks, SPAN, SPAN), F32), sds((chunks, SPAN, SPAN), F32), sds((ext, 8), F32),
            sds((8, 128), F32), sds((rows, 128), BF), sds((rows, 128), BF), sds((rows, 128), BF),
            sds((rows, 128), BF),
        ],
        scratch_shapes=[pltpu.VMEM((ext, WIDE), F32), pltpu.VMEM((docs.shape[1], 1), F32)],
        compiler_params=params(),
        cost_estimate=cost(8),
        name="keys_queries",
    )(xk, xg, *wc, *packs, taps, hp, docs)

    def columns(height, base=0):
        return pl.BlockSpec((height, WIDE), lambda i: (0, i + base))

    def states(base=0):
        return pl.BlockSpec((chunks, STATE, WIDE), lambda i: (0, 0, i + base))

    def cumt_spec(base=0):
        return pl.BlockSpec((1, GROUP, rows), lambda i: (i + base, 0, 0))

    run, wo_top = lax.optimization_barrier((run, out_weight[:wide_rows]))
    wo_a = gather_first(wo_top)
    proj_v, act, slope_v, adds, last = pl.pallas_call(
        state_kernel,
        grid=(GROUPS,),
        in_specs=whole_x + [columns(quarter)] * 4 + [
            columns(8), whole((ext, 8)), head_table, head_table, whole((WIDE, rows)),
        ],
        out_specs=[columns(ext), columns(rows), columns(rows), states(), columns(STATE)],
        out_shape=[
            sds((ext, INNER), BF), sds((rows, INNER), BF), sds((rows, INNER), BF),
            sds((chunks, STATE, INNER), BF), sds((STATE, INNER), BF),
        ],
        scratch_shapes=[pltpu.VMEM((ext, WIDE), F32)],
        compiler_params=params(),
        cost_estimate=cost(20),
        name="values_states",
    )(xk, xg, *wc, taps, masks, give2, cum, turned)

    wg_far, wo_far, last, act, adds, proj_v, slope_v = lax.optimization_barrier(
        (wg[2], wo_a[2], last, act, adds, proj_v, slope_v)
    )
    wg = wg[:2] + (wg_far, swap(wg_far, "shard", 1))
    wo_a = wo_a[:2] + (wo_far, swap(wo_far, "shard", 1))
    run_prev, run_next = passed_along(run, 1), passed_along(run, -1)
    near, far = passed_along(last, 1), passed_along(last, 2)

    inside, gate = pl.pallas_call(
        inside_kernel,
        grid=(GROUPS,),
        in_specs=whole_x + [columns(quarter)] * 4 + [
            columns(rows), head_table, head_table, cumt_spec(), whole((chunks, SPAN, SPAN)),
            whole((8, 128)),
        ],
        out_specs=[columns(rows), columns(rows)],
        out_shape=[sds((rows, INNER), BF), sds((rows, INNER), BF)],
        compiler_params=params(),
        cost_estimate=cost(20),
        name="scan_inside",
    )(xk, xg, *wg, act, step2, cum, cumt, mix, hp)

    near, far, run_prev, inside, gate, wo_low = lax.optimization_barrier(
        (near, far, run_prev, inside, gate, out_weight[wide_rows:])
    )
    wo_b = gather_first(wo_low)
    y, mixed, rms, into = pl.pallas_call(
        mixed_kernel,
        grid=(GROUPS,),
        in_specs=[
            columns(rows), columns(rows), whole((rows, WIDE)), head_table, head_table, states(),
            columns(STATE), columns(STATE), whole((8, 128)), whole((1, INNER)),
        ],
        out_specs=[columns(rows), whole((rows, INNER)), head_table, columns(STATE)],
        out_shape=[
            sds((rows, INNER), BF), sds((rows, INNER), BF), sds((rows, 128), F32),
            sds((STATE, INNER), F32),
        ],
        scratch_shapes=[
            pltpu.VMEM((GROUPS, rows, WIDE), F32), pltpu.VMEM((rows, 128), F32),
        ],
        compiler_params=params(),
        cost_estimate=cost(10),
        name="scan_gate",
    )(inside, gate, kq, enter2, cum, adds, near, far, run_prev, gate_row)
    wo_far, y, mixed, rms, into = lax.optimization_barrier((wo_b[2], y, mixed, rms, into))
    wo_b = wo_b[:2] + (wo_far, swap(wo_far, "shard", 1))
    wo = [part for both in zip(wo_a, wo_b) for part in both]

    def by_chunk(width):
        return pl.BlockSpec((SPAN, width), lambda c: (c, 0))

    grad_out = mm_tn(mixed, cotangent).astype(BF)
    grad_out, cum_then = lax.optimization_barrier((grad_out, cum))
    sum_out = lax.psum_scatter(grad_out, "shard", scatter_dimension=0, tiled=True)
    wo_specs = [whole((wide_rows, model))] * 8

    dy, dgate, dgain, dskip, radds, first = pl.pallas_call(
        gate_back_kernel,
        grid=(chunks,),
        in_specs=[scalar(), by_chunk(model)] + wo_specs + [
            by_chunk(INNER), by_chunk(INNER), by_chunk(INNER), by_chunk(128), whole((1, INNER)),
            by_chunk(INNER),
            pl.BlockSpec((WIDE, SPAN), lambda c: (0, c)), by_chunk(128), by_chunk(128),
        ],
        out_specs=[
            by_chunk(INNER), by_chunk(INNER), whole((8, INNER)), whole((8, INNER)),
            pl.BlockSpec((1, STATE, INNER), lambda c: (c, 0, 0)), whole((STATE, INNER)),
        ],
        out_shape=[
            sds((rows, INNER), BF), sds((rows, INNER), BF), sds((8, INNER), F32),
            sds((8, INNER), F32), sds((chunks, STATE, INNER), BF), sds((STATE, INNER), BF),
        ],
        scratch_shapes=[
            pltpu.VMEM((SPAN, INNER), F32), pltpu.VMEM((8, 128), F32),
            pltpu.VMEM((STATE, INNER), F32),
        ],
        compiler_params=params(),
        cost_estimate=cost(22),
        name="gate_back",
    )(at_me, cotangent, *wo, y, gate, mixed, rms, gate_row, act, turned, enter2, cum_then)

    grad_gate = mm_tn(plain, dgate).astype(BF)
    near, far = passed_along(first, -1), passed_along(first, -2)
    grad_gate, mixed_then = lax.optimization_barrier((grad_gate, mixed))
    sum_gate = lax.psum_scatter(grad_gate, "shard", scatter_dimension=0, tiled=True)
    output, part = pl.pallas_call(
        rows_kernel,
        grid=(chunks,),
        in_specs=[scalar(), by_chunk(INNER), by_chunk(model), by_chunk(INNER)] + wo_specs
        + [whole((quarter, INNER))] * 4,
        out_specs=[by_chunk(model), by_chunk(model)],
        out_shape=[sds((rows, model), BF), sds((rows, model), F32)],
        compiler_params=params(),
        cost_estimate=cost(18),
        name="rows_out",
    )(at_me, mixed_then, tokens, dgate, *wo, *wg)
    near, far, output, part, run_next, sum_out = lax.optimization_barrier(
        (near, far, output, part, run_next, sum_out)
    )
    sum_out = lax.psum(sum_out, "rep")

    dprojs, dtaps, partials = [], [], []
    sums = []

    def add_sum(parts, scattered):
        grad = parts[0] if len(parts) == 1 else jnp.concatenate(parts, axis=1)
        sums.append(RowSum(mm_tn(xk, grad), mm_tn(xg, grad).astype(BF), scattered))

    cum_then, output = lax.optimization_barrier((cum, output))
    for k, count in enumerate(CALLS):
        base = sum(CALLS[:k])
        width = count * WIDE
        dproj, dtap, *rest = pl.pallas_call(
            partial(scan_back_kernel, base),
            grid=(count,),
            in_specs=[
                whole((rows, WIDE)), whole((chunks, SPAN, SPAN)), head_table, head_table,
                head_table, head_table, cumt_spec(base), columns(rows, base), columns(rows, base),
                states(base), states(base), columns(STATE, base), columns(STATE, base),
                columns(STATE, base), whole((8, 128)), whole((8, 128)), columns(ext, base),
                columns(rows, base), columns(8, base), whole((ext, 8)),
            ],
            out_specs=[
                columns(ext), columns(8), whole((rows, WIDE)), head_table,
                whole((GROUP * count, rows)), whole((8 * chunks, 128)), head_table,
            ],
            out_shape=[
                sds((ext, width), BF), sds((8, width), F32), sds((rows, WIDE), F32),
                sds((rows, 128), F32), sds((GROUP * count, rows), F32),
                sds((8 * chunks, 128), F32), sds((rows, 128), F32),
            ],
            scratch_shapes=[
                pltpu.VMEM((ext + 8, WIDE), F32), pltpu.VMEM((chunks, SPAN, SPAN), F32),
                pltpu.VMEM((chunks, STATE, WIDE), F32),
            ],
            compiler_params=params(),
            cost_estimate=cost(15),
            name="scan_back",
        )(kq, mixt, step2, enter2, leave2, cum_then, cumt, act, dy, adds, radds, into, near, far,
          run_next, hp, proj_v, slope_v, taps, masks)
        if k == 0:
            sum_gate, dproj = lax.optimization_barrier((sum_gate, dproj))
            sum_gate = lax.psum(sum_gate, "rep")
        dproj, dtap, rest = ordered((dproj, dtap, rest), *sums)
        dprojs.append(dproj)
        dtaps.append(dtap)
        partials.extend(rest)
        add_sum([dproj], 2 if k == 0 else 1)
        cum_then, raw_then = ordered((cum, raw), sums[-1])

    tail = WIDE + 128
    dlast, dtap, head_sums = pl.pallas_call(
        last_kernel,
        grid=(1,),
        in_specs=[
            spec
            for count in CALLS
            for spec in (
                whole((rows, WIDE)), head_table, whole((GROUP * count, rows)),
                whole((8 * chunks, 128)), head_table,
            )
        ] + [
            head_table, head_table, whole((8, 128)), whole((ext, WIDE)), whole((rows, WIDE)),
            pl.BlockSpec((8, WIDE), lambda i: (0, kq_block)), whole((ext, 8)),
        ],
        out_specs=[whole((ext, tail)), whole((8, WIDE)), whole((8, 128))],
        out_shape=[sds((ext, tail), BF), sds((8, WIDE), F32), sds((8, 128), F32)],
        scratch_shapes=[pltpu.VMEM((ext + 8, WIDE), F32)],
        compiler_params=params(),
        cost_estimate=cost(8),
        name="last_back",
    )(*partials, raw_then, step, hp, proj_kq, slope_kq, taps, masks)
    dlast, dtap, head_sums = ordered((dlast, dtap, head_sums), *sums)
    dprojs.append(dlast)
    dtaps.append(dtap)

    add_sum(dprojs[3:], 0)
    part = ordered(part, sums[3])
    heads = jnp.concatenate([p[:HALO] for p in dprojs[:3]] + [dlast[:HALO, :WIDE]], axis=1)
    back = passed_along(heads, -1)
    value_part = pl.pallas_call(
        values_kernel,
        grid=(chunks,),
        in_specs=[scalar(), by_chunk(model)]
        + [whole((ext, count * WIDE)) for count in CALLS]
        + [pl.BlockSpec((quarter, INNER), lambda c: (0, 0))] * 4,
        out_specs=by_chunk(model),
        out_shape=sds((rows, model), F32),
        compiler_params=params(),
        cost_estimate=cost(10),
        name="values_back",
    )(at_me, part, *dprojs[:3], *wc)
    value_part, back = ordered((value_part, back), *sums)
    grad_tokens, g_norm = pl.pallas_call(
        tokens_kernel,
        grid=(chunks,),
        in_specs=[scalar(), by_chunk(model), by_chunk(model), whole((1, model)), by_chunk(model)]
        + [whole((ext, tail)), whole((HALO, conv))]
        + [whole((quarter, conv))] * 4
        + [whole(packed.shape)] * 4,
        out_specs=[by_chunk(model), whole((8, model))],
        out_shape=[sds((rows, model), F32), sds((8, model), F32)],
        scratch_shapes=[pltpu.VMEM((SPAN, model), F32)],
        compiler_params=params(),
        cost_estimate=cost(8),
        name="tokens_back",
    )(at_me, tokens, cotangent, norm_row, value_part, dlast, back, *wc, *packs)

    grad_tokens, g_norm = ordered((grad_tokens, g_norm), *sums)
    dtaps = jnp.concatenate(dtaps, axis=1)
    g_skip = jnp.sum(dskip[0].reshape(HEADS, HEAD_DIM), axis=1)
    parts = (
        g_norm[0], dtaps[:KW].T.reshape(-1), dtaps[KW], head_sums[1, :HEADS],
        head_sums[0, :HEADS], g_skip, dgain[0],
    )
    total, sum_out, sum_gate = reduce_small(jnp.concatenate(parts), sum_out, sum_gate)
    sums = [one.result() for one in sums]
    outs, start = [], 0
    for part in parts:
        size = part.shape[0] // 4
        outs.append(lax.dynamic_slice(total, (start + me * size,), (size,)))
        start += part.shape[0]
    s_norm, s_conv, s_cbias, s_step, s_decay, s_skip, s_gate = outs
    s_in = jnp.concatenate([sum_gate.astype(F32)] + sums[:3] + [sums[3][:, :WIDE]], axis=1)
    s_dt = sums[3][:, WIDE : WIDE + HEADS]
    return (
        output, grad_tokens, s_norm, s_in, s_dt, s_conv.reshape(-1, KW), s_cbias, s_step, s_decay,
        s_skip, s_gate, sum_out.astype(F32),
    )


def solution(mesh):
    spread = P(("rep", "shard"), None)
    row = P("shard")
    table = P("shard", None)
    return jax.shard_map(
        on_device,
        mesh=mesh,
        in_specs=(
            spread, P(("rep", "shard")), row, table, table, table, row, row, row, row, row, table,
            spread,
        ),
        out_specs=(
            spread, spread, row, table, table, table, row, row, row, row, row, table,
        ),
        check_vma=False,
    )
```
